32 devices in a mesh: segment: 4 (over x, core), graph: 8 (over z, y).
Axes of the slice: x: 2, y: 2, z: 4, core: 2. Of those that a mesh axis runs over, the one named last changes fastest.
Arguments:
- state: float32 [4, 4096, 1024], P('segment', 'graph'), may hold values from -6 to 6
- initial: float32 [4, 4096, 1024], P('segment', 'graph'), may hold values from -6 to 6
- fresh: float32 [4096, 1024], P('graph'), may hold values from -6 to 6
- weights: float32 [4, 1024, 1024], P('segment'), may hold values from -0.1875 to 0.1875
- wants: int32 [8, 4, 1], P('graph'), may hold values from 0 to 3
- adj_slot: int32 [32, 4], P('graph'), may hold values from 0 to 7, as said below
- adj_count: int32 [32], P('graph'), may hold values from 2 to 4, as said below
- adj_vals: float32 [32, 4, 128, 128], P('graph'), may hold values from -0.25 to 0.25
Outputs:
- handed: float32 [4, 4096, 1024], P('segment', 'graph')
- advanced: float32 [4, 4096, 1024], P('segment', 'graph')
The draws below stay inside these ranges and needn't reach their ends.
Inputs may be any that keep to these rules, and one draw needn't show every extreme that they name: `adj_slot`: every entry of a destination block's row at k < 2 names a slot past the partition's own blocks, and every such slot of a partition is named at some k < 2 of one of its blocks. `adj_count`: each partition has a block with exactly 4 nonzero blocks.
All inputs are finite; a program needn't handle non-finite values.
Results may differ from the reference program's by a relative error of at most 0.0001.
Values sent between devices are 32-bit elements; how exact they have to be, the bound alone decides.
No kernel may reach another device: no remote copies, remote signals or barrier semaphores. Data moves between devices by JAX's collectives and lax.ppermute only.
A program may use at most 128 MiB of HBM per device.

```python
import jax
import jax.numpy as jnp
from jax import lax

D = 1024
BLK = 128
V_DEV = 512
KMAX = 4
REACH = 2
CAP = 1
NB = 4
VBLK = 32
N = 4096
N_SEGMENT = 4
N_GRAPH = 8


def draw_adj_slot(key, part):
    key_base = jax.random.fold_in(key, 11)
    key_shift = jax.random.fold_in(key, 12)
    received_count = 2 * REACH * CAP
    base = jax.random.randint(key_base, (N_GRAPH, NB, KMAX), 0, NB + received_count).astype(jnp.int32)
    rotation = jax.random.randint(key_shift, (N_GRAPH, 1), 0, received_count).astype(jnp.int32)
    positions = jnp.arange(2 * NB, dtype=jnp.int32)[None, :]
    forced = NB + (positions + rotation) % received_count
    forced = forced.reshape(N_GRAPH, NB, 2)
    merged = jnp.concatenate([forced, base[:, :, 2:]], axis=2)
    return merged.reshape(VBLK, KMAX).astype(jnp.int32)


def draw_adj_count(key, part):
    key_base = jax.random.fold_in(key, 21)
    key_row = jax.random.fold_in(key, 22)
    counts = jax.random.randint(key_base, (N_GRAPH, NB), 2, KMAX + 1).astype(jnp.int32)
    chosen_row = jax.random.randint(key_row, (N_GRAPH, 1), 0, NB).astype(jnp.int32)
    columns = jnp.arange(NB, dtype=jnp.int32)[None, :]
    counts = jnp.where(columns == chosen_row, KMAX, counts)
    return counts.reshape(VBLK).astype(jnp.int32)


def with_ends(result, own_key, smallest, top_value):
    longest = result.shape.index(max(result.shape))
    spots = []
    for shift in (0, 1):
        where = [jax.random.randint(jax.random.fold_in(own_key, axis), (), 0, length) for axis, length in enumerate(result.shape)]
        where[longest] = (where[longest] + shift) % result.shape[longest]
        spots.append(tuple(where))
    return result.at[spots[0]].set(smallest).at[spots[1]].set(top_value)


def level_of(stream_key, extent, cuts, least, top_value):
    factor_of = 1.0
    for dim, blocks in cuts:
        steps = jax.random.uniform(jax.random.fold_in(jax.random.fold_in(stream_key, 6), dim), (blocks,), jnp.float32, least / len(cuts), top_value / len(cuts))
        factor_of = factor_of * jnp.repeat(jnp.exp(steps), extent[dim] // blocks).reshape((-1,) + (1,) * (len(extent) - 1 - dim))
    return factor_of


def bell_draw(stream_key, extent, width, bound, pieces=(), kind=jnp.bfloat16):
    result = width * jax.random.normal(stream_key, extent, jnp.float32)
    if pieces:
        result = result * level_of(stream_key, extent, pieces, -0.22, 0.18)
    return jnp.clip(result, -bound, bound).astype(kind)


def setup_inputs(seed: int = 0) -> dict:
    splits = jax.random.split(jax.random.key(seed), 9)
    return {
        "state": bell_draw(splits[0], (N_SEGMENT, N, D), 1.0, 6.0, ((0, 4), (1, 8)), jnp.float32),
        "initial": bell_draw(splits[1], (N_SEGMENT, N, D), 1.0, 6.0, ((0, 4), (1, 8)), jnp.float32),
        "fresh": bell_draw(splits[2], (N, D), 1.0, 6.0, ((0, 8),), jnp.float32),
        "weights": bell_draw(splits[3], (N_SEGMENT, D, D), D ** -0.5, 0.1875, ((0, 4),), jnp.float32),
        "wants": with_ends(jax.random.randint(splits[4], (N_GRAPH, 2 * REACH, CAP), 0, NB), jax.random.fold_in(splits[4], 1), 0, NB - 1).astype(jnp.int32),
        "adj_slot": draw_adj_slot(jax.random.fold_in(splits[8], 71), 0),
        "adj_count": draw_adj_count(jax.random.fold_in(splits[8], 71), 0),
        "adj_vals": bell_draw(splits[7], (VBLK, KMAX, BLK, BLK), (BLK * KMAX) ** -0.5, 0.25, ((0, 8),), jnp.float32),
    }


def offset_list():
    found = []
    for radius in range(1, REACH + 1):
        found.append(radius)
        found.append(-radius)
    return found


def apply_layer(feats, first_feats, weight, layer_index, wants, adj_slot, adj_count, adj_vals):
    parts = N_GRAPH
    nblocks = V_DEV // BLK
    row_blocks = feats.reshape(parts, nblocks, BLK, D)
    partition = jnp.arange(parts, dtype=jnp.int32)
    received = []
    for position, shift_by in enumerate(offset_list()):
        source = partition - shift_by
        valid = ((source >= 0) & (source < parts)).astype(jnp.float32)
        clipped = jnp.clip(source, 0, parts - 1).astype(jnp.int32)
        chosen = wants[:, position, :]
        picked = row_blocks[clipped[:, None], chosen]
        received.append(picked * valid[:, None, None, None])
    sources = jnp.concatenate([row_blocks] + received, axis=1)
    slots = adj_slot.reshape(parts, nblocks, KMAX)
    selected = sources[partition[:, None, None], slots]
    live = (jnp.arange(KMAX, dtype=jnp.int32)[None, None, :] < adj_count.reshape(parts, nblocks)[:, :, None]).astype(jnp.float32)
    values = adj_vals.reshape(parts, nblocks, KMAX, BLK, BLK) * live[:, :, :, None, None]
    agg = jnp.einsum("gbkij,gbkjd->gbid", values, selected, precision=lax.Precision.HIGHEST).reshape(parts * nblocks * BLK, D)
    mixed = 0.9 * agg + 0.1 * first_feats
    beta = jnp.log(0.5 / (layer_index + 1.0) + 1.0)
    product = jnp.dot(mixed, weight, precision=lax.Precision.HIGHEST, preferred_element_type=jnp.float32)
    return jax.nn.relu((1.0 - beta) * mixed + beta * product)


def reference(state, initial, fresh, weights, wants, adj_slot, adj_count, adj_vals):
    handed_list = []
    for section in range(N_SEGMENT):
        handed_list.append(apply_layer(state[section], initial[section], weights[section], float(section), wants, adj_slot, adj_count, adj_vals))
    advanced_list = []
    for section in range(N_SEGMENT):
        if section == 0:
            feats, first_feats = fresh, fresh
        else:
            feats, first_feats = handed_list[section - 1], initial[section - 1]
        advanced_list.append(apply_layer(feats, first_feats, weights[section], float(section), wants, adj_slot, adj_count, adj_vals))
    return jnp.stack(handed_list), jnp.stack(advanced_list)
```

```python
import functools

import jax
import jax.numpy as jnp
from jax import lax
from jax.experimental import pallas as pl
from jax.experimental.pallas import tpu as pltpu
from jax.sharding import PartitionSpec as P

BLK = 128
REACH = 2
F32 = jnp.float32
BF16 = jnp.bfloat16
SWAPS = ((1, 0), (2, 0), (2, 1), (1, 1))
VMEM = pl.BlockSpec(memory_space=pltpu.VMEM)
SMEM = pl.BlockSpec(memory_space=pltpu.SMEM)
HBM = pl.BlockSpec(memory_space=pl.ANY)
ONE = pltpu.SemaphoreType.DMA


def swap(value, stride, phase):
    peers = lax.axis_size("graph")
    pairs = []
    for low in range(peers - stride):
        if (low // stride) % 2 == phase:
            pairs += [(low, low + stride), (low + stride, low)]
    return lax.ppermute(value, "graph", sorted(pairs))


def hand_on(value):
    peers = lax.axis_size("segment")
    return lax.ppermute(value, "segment", [(i, (i + 1) % peers) for i in range(peers)])


def halves(value):
    high = value.astype(BF16)
    return high, (value - high.astype(F32)).astype(BF16)


def dot3(a, b):
    times = functools.partial(jnp.dot, preferred_element_type=F32)
    return times(a[0], b[0]) + (times(a[0], b[1]) + times(a[1], b[0]))


def call(kernel, outs, in_specs, out_specs, flops=0, nbytes=0, scratch=(), grid=None, vmem=32):
    extra = {} if grid is None else {"grid": grid}
    return pl.pallas_call(
        kernel,
        out_shape=outs,
        in_specs=in_specs,
        out_specs=out_specs,
        scratch_shapes=list(scratch),
        cost_estimate=pl.CostEstimate(flops=flops, bytes_accessed=nbytes, transcendentals=0),
        compiler_params=pltpu.CompilerParams(vmem_limit_bytes=vmem * 2**20),
        **extra,
    )


def dense_kernel(place_ref, slot_ref, count_ref, vals_ref, high_ref, low_ref, total):
    total[...] = jnp.zeros_like(total)
    blocks, most = vals_ref.shape[:2]
    for b in range(blocks):
        for k in range(most):
            slot = slot_ref[b, k]
            past = jnp.maximum(slot - blocks, 0)
            column = jnp.where(slot < blocks, slot, blocks + place_ref[past])
            scale = jnp.where(k < count_ref[b], 0.9, 0.0).astype(F32)
            where = pl.ds(pl.multiple_of(column * BLK, BLK), BLK)
            total[b * BLK : (b + 1) * BLK, where] += scale * vals_ref[b, k]
    high, low = halves(total[...])
    high_ref[...] = high
    low_ref[...] = low


def dense(place, slots, counts, vals):
    rows = vals.shape[0] * BLK
    width = rows + 2 * REACH * BLK
    shape = jax.ShapeDtypeStruct((rows, width), BF16)
    return call(
        dense_kernel,
        (shape, shape),
        [SMEM, SMEM, SMEM, VMEM],
        (VMEM, VMEM),
        nbytes=4 * vals.size + 4 * rows * width,
        scratch=[pltpu.VMEM((rows, width), F32)],
    )(place, slots, counts, vals)


def pick_kernel(index_ref, *refs, count):
    got, source, outs, sem = refs[:count], refs[count], refs[count + 1 : -1], refs[-1]
    copies = []
    for i in range(count):
        row = pl.multiple_of(got[i][index_ref[i]] * BLK, BLK)
        copies.append(pltpu.make_async_copy(source.at[pl.ds(row, BLK)], outs[i], sem.at[i]))
    for copy in copies:
        copy.start()
    for copy in copies:
        copy.wait()


def pick(index, got, source):
    count = len(got)
    shape = jax.ShapeDtypeStruct((BLK, source.shape[1]), F32)
    return call(
        functools.partial(pick_kernel, count=count),
        (shape,) * count,
        [SMEM] * (1 + count) + [HBM],
        (HBM,) * count,
        nbytes=8 * count * BLK * source.shape[1],
        scratch=[ONE((count,))],
    )(index, *got, source)


def own_kernel(high_ref, low_ref, feats_ref, first_ref, out_ref):
    a = (high_ref[...], low_ref[...])
    out_ref[...] = dot3(a, halves(feats_ref[...])) + 0.1 * first_ref[...]


def own_part(adj, feats, first, column=0, width=None, tile=256):
    rows = feats.shape[0]
    width = feats.shape[1] if width is None else width
    start = column // tile
    spec = pl.BlockSpec((rows, rows), lambda i: (0, 0))
    cut = pl.BlockSpec((rows, tile), lambda i: (0, start + i))
    return call(
        own_kernel,
        jax.ShapeDtypeStruct((rows, width), F32),
        [spec, spec, cut, cut],
        pl.BlockSpec((rows, tile), lambda i: (0, i)),
        flops=6 * rows * rows * width,
        nbytes=12 * rows * width + 4 * rows * rows,
        grid=(width // tile,),
    )(*adj, feats, first)


def product_kernel(beta_ref, high_ref, low_ref, base_ref, weight_ref, *refs, near, relu):
    came, out_ref, mixed, total = refs[:near], refs[near], refs[near + 1], refs[near + 2]
    step, last = pl.program_id(0), pl.num_programs(0) - 1
    tile = weight_ref.shape[0]
    part = base_ref[...]
    if near:
        received = jnp.concatenate([r[...] for r in came], axis=0)
        part = part + dot3((high_ref[...], low_ref[...]), halves(received))
    mixed[:, pl.ds(pl.multiple_of(step * tile, tile), tile)] = part
    term = dot3(halves(part), halves(weight_ref[...]))

    @pl.when(step == 0)
    def _():
        total[...] = term

    @pl.when(step > 0)
    def _():
        total[...] += term

    @pl.when(step == last)
    def _():
        beta = beta_ref[0]
        value = (1.0 - beta) * mixed[...] + beta * total[...]
        out_ref[...] = jnp.maximum(value, 0.0) if relu else value


def product(beta, adj, base, weight, received, column, relu, tile=256):
    rows, depth = base.shape
    width = weight.shape[1]
    near = len(received)
    span = max(near, 1) * BLK
    at = column // span
    assert at * span == column
    spec = pl.BlockSpec((rows, span), lambda i: (0, at))
    return call(
        functools.partial(product_kernel, near=near, relu=relu),
        jax.ShapeDtypeStruct((rows, width), F32),
        [SMEM, spec, spec, pl.BlockSpec((rows, tile), lambda i: (0, i)), pl.BlockSpec((tile, width), lambda i: (i, 0))]
        + [pl.BlockSpec((BLK, tile), lambda i: (0, i))] * near,
        pl.BlockSpec((rows, width), lambda i: (0, 0)),
        flops=6 * rows * depth * width,
        nbytes=4 * (depth * width + 2 * rows * width),
        scratch=[pltpu.VMEM((rows, depth), F32), pltpu.VMEM((rows, width), F32)],
        grid=(depth // tile,),
        vmem=40,
    )(beta, *adj, base, weight, *received)


def add_kernel(high_ref, low_ref, base_ref, *refs):
    came, out_ref = refs[:-1], refs[-1]
    received = jnp.concatenate([r[...] for r in came], axis=0)
    out_ref[...] = base_ref[...] + dot3((high_ref[...], low_ref[...]), halves(received))


def add_received(adj, base, received, column, tile=256):
    rows, width = base.shape
    span = len(received) * BLK
    at = column // span
    spec = pl.BlockSpec((rows, span), lambda i: (0, at))
    return call(
        add_kernel,
        jax.ShapeDtypeStruct((rows, width), F32),
        [spec, spec, pl.BlockSpec((rows, tile), lambda i: (0, i))]
        + [pl.BlockSpec((BLK, tile), lambda i: (0, i))] * len(received),
        pl.BlockSpec((rows, tile), lambda i: (0, i)),
        flops=6 * rows * span * width,
        nbytes=8 * rows * width,
        grid=(width // tile,),
    )(*adj, base, *received)


def shards(state, initial, fresh, weights, wants, adj_slot, adj_count, adj_vals):
    section = lax.axis_index("segment")
    part = lax.axis_index("graph")
    beta = jnp.log(0.5 / (section.astype(F32) + 1.0) + 1.0).reshape(1)
    last = section == lax.axis_size("segment") - 1
    feats, first, weight = state[0], initial[0], weights[0]
    rows, depth = feats.shape
    half = depth // 2
    asks = wants.reshape(wants.shape[1])

    place = []
    for position in range(2 * REACH):
        stride = position // 2 + 1
        low = (part // stride) % 2 == 0
        phase = jnp.where(low, 1 - position % 2, position % 2)
        place.append(jnp.where(phase == 0, SWAPS.index((stride, 0)), SWAPS.index((stride, 1))))
    place = jnp.stack(place).astype(jnp.int32)
    index = []
    for stride, phase in SWAPS:
        low = (part // stride) % 2 == phase
        index.append(jnp.where(low, 2 * stride - 2, 2 * stride - 1))
    index = jnp.stack(index).astype(jnp.int32)

    got = [swap(asks, *kind) for kind in SWAPS]
    adj = dense(place, adj_slot, adj_count, adj_vals)

    sent = [pick(index[i : i + 1], got[i : i + 1], feats)[0] for i in range(len(SWAPS))]
    came = [swap(value, *kind) for value, kind in zip(sent, SWAPS)]
    next_first = jnp.where(last, fresh, first)
    first_left = hand_on(next_first[:, :half])
    mixed = own_part(adj, feats, first)
    first_out = product(beta, adj, mixed, weight, came, rows, True)

    next_feats = jnp.where(last, fresh, first_out)
    left = hand_on(next_feats[:, :half])
    right = next_feats[:, half:]
    came_right = [swap(value, *kind) for value, kind in zip(pick(index, got, right), SWAPS)]
    mixed_right = own_part(adj, right, next_first[:, half:])
    mixed_right = hand_on(add_received(adj, mixed_right, came_right, rows))
    came_left = [swap(value, *kind) for value, kind in zip(pick(index, got, left), SWAPS)]
    mixed_left = own_part(adj, left, first_left)
    mixed_left = add_received(adj, mixed_left, came_left, rows)
    base = jnp.concatenate([mixed_left, mixed_right], axis=1)
    second_out = product(beta, adj, base, weight, [], rows, True)
    return first_out[None], second_out[None]


def solution(mesh):
    return jax.shard_map(
        shards,
        mesh=mesh,
        in_specs=(
            P("segment", "graph", None),
            P("segment", "graph", None),
            P("graph", None),
            P("segment", None, None),
            P("graph", None, None),
            P("graph", None),
            P("graph"),
            P("graph", None, None, None),
        ),
        out_specs=(P("segment", "graph", None), P("segment", "graph", None)),
        check_vma=False,
    )
```

```python
import functools

import jax
import jax.numpy as jnp
from jax import lax
from jax.experimental import pallas as pl
from jax.experimental.pallas import tpu as pltpu
from jax.sharding import PartitionSpec as P

BLK = 128
REACH = 2
F32 = jnp.float32
BF16 = jnp.bfloat16
SWAPS = ((1, 0), (2, 0), (2, 1), (1, 1))
VMEM = pl.BlockSpec(memory_space=pltpu.VMEM)
SMEM = pl.BlockSpec(memory_space=pltpu.SMEM)
HBM = pl.BlockSpec(memory_space=pltpu.HBM)
ONE = pltpu.SemaphoreType.DMA


def swap(value, stride, phase):
    peers = lax.axis_size("graph")
    pairs = []
    for low in range(peers - stride):
        if (low // stride) % 2 == phase:
            pairs += [(low, low + stride), (low + stride, low)]
    return lax.ppermute(value, "graph", sorted(pairs))


def hand_on(value):
    peers = lax.axis_size("segment")
    return lax.ppermute(value, "segment", [(i, (i + 1) % peers) for i in range(peers)])


def halves(value):
    high = value.astype(BF16)
    return high, (value - high.astype(F32)).astype(BF16)


def dot3(a, b):
    times = functools.partial(jnp.dot, preferred_element_type=F32)
    return times(a[0], b[0]) + (times(a[0], b[1]) + times(a[1], b[0]))


def call(kernel, args, in_specs, outs, flops=0, nbytes=0, scratch=(), after=(), vmem=16):
    count = len(args)

    def body(*refs):
        kernel(*refs[:count], *refs[count + len(after) :])

    return pl.pallas_call(
        body,
        out_shape=outs,
        in_specs=list(in_specs) + [VMEM] * len(after),
        out_specs=tuple(VMEM if isinstance(out, jax.ShapeDtypeStruct) else HBM for out in outs),
        scratch_shapes=list(scratch),
        cost_estimate=pl.CostEstimate(flops=flops, bytes_accessed=nbytes, transcendentals=0),
        compiler_params=pltpu.CompilerParams(vmem_limit_bytes=vmem * 2**20),
    )(*args, *after)


def vmem(*shape, dtype=F32):
    return jax.ShapeDtypeStruct(shape, dtype)


def prepare_kernel(place_ref, slot_ref, count_ref, index_ref, got_ref, *refs, kind):
    vals_ref, feats_ref, high_ref, low_ref, sent_ref, held, total, sem = refs
    copies = [pltpu.make_async_copy(vals_ref, held, sem.at[0])]
    row = pl.multiple_of(got_ref[index_ref[kind]] * BLK, BLK)
    copies.append(pltpu.make_async_copy(feats_ref.at[pl.ds(row, BLK)], sent_ref, sem.at[1]))
    for copy in copies:
        copy.start()
    total[...] = jnp.zeros_like(total)
    blocks, most = held.shape[:2]
    copies[0].wait()
    for b in range(blocks):
        for k in range(most):
            slot = slot_ref[b, k]
            past = jnp.maximum(slot - blocks, 0)
            column = jnp.where(slot < blocks, slot, blocks + place_ref[past])
            scale = jnp.where(k < count_ref[b], 0.9, 0.0).astype(F32)
            where = pl.ds(pl.multiple_of(column * BLK, BLK), BLK)
            total[b * BLK : (b + 1) * BLK, where] += scale * held[b, k]
    high, low = halves(total[...])
    high_ref[...] = high
    low_ref[...] = low
    copies[1].wait()


def in_hbm(value):
    return pltpu.with_memory_space_constraint(value, pltpu.HBM)


def prepare(kind, place, slots, counts, index, got, vals, feats, after=()):
    rows, width = feats.shape
    span = rows + 2 * REACH * BLK
    return call(
        functools.partial(prepare_kernel, kind=kind),
        (place, slots, counts, index, got[kind], in_hbm(vals), in_hbm(feats)),
        [SMEM] * 5 + [HBM] * 2,
        (vmem(rows, span, dtype=BF16),) * 2 + (vmem(BLK, width),),
        nbytes=4 * vals.size + 4 * rows * span,
        scratch=[pltpu.VMEM(vals.shape, F32), pltpu.VMEM((rows, span), F32), ONE((2,))],
        after=after,
    )


def pick_kernel(index_ref, *refs, kinds):
    count = len(kinds)
    got, source, outs, sem = refs[:count], refs[count], refs[count + 1 : -1], refs[-1]
    copies = []
    for i, kind in enumerate(kinds):
        row = pl.multiple_of(got[i][index_ref[kind]] * BLK, BLK)
        copies.append(pltpu.make_async_copy(source.at[pl.ds(row, BLK)], outs[i], sem.at[i]))
        copies[-1].start()
    for copy in copies:
        copy.wait()


def pick(kinds, index, got, source, after=()):
    return call(
        functools.partial(pick_kernel, kinds=kinds),
        (index, *[got[k] for k in kinds], in_hbm(source)),
        [SMEM] * (1 + len(kinds)) + [HBM],
        (vmem(BLK, source.shape[1]),) * len(kinds),
        nbytes=8 * BLK * source.shape[1] * len(kinds),
        scratch=[ONE((len(kinds),))],
        after=after,
    )


def wanted(kinds, index_ref, got, source_ref, outs):
    for kind, got_ref, out_ref in zip(kinds, got, outs):
        row = pl.multiple_of(got_ref[index_ref[kind]] * BLK, BLK)
        out_ref[...] = source_ref[pl.ds(row, BLK), :]


def choose_kernel(index_ref, *refs, kinds):
    count = len(kinds)
    wanted(kinds, index_ref, refs[:count], refs[count], refs[count + 1 :])


def choose(kinds, index, got, source, after=()):
    return call(
        functools.partial(choose_kernel, kinds=kinds),
        (index, *[got[k] for k in kinds], source),
        [SMEM] * (1 + len(kinds)) + [VMEM],
        (vmem(BLK, source.shape[1]),) * len(kinds),
        nbytes=8 * len(kinds) * BLK * source.shape[1],
        after=after,
    )


def times_adj(high_ref, low_ref, at, value):
    cut = slice(at, at + value.shape[0])
    return dot3((high_ref[:, cut], low_ref[:, cut]), halves(value))


def stacked(refs):
    return jnp.concatenate([ref[...] for ref in refs], axis=0)


def early_kernel(beta_ref, last_ref, high_ref, low_ref, weight_ref, *refs):
    came, sources, (out_ref, left_ref, right_ref), refs = refs[:-10], refs[-10:-7], refs[-7:-4], refs[-4:]
    held, sem = refs[:3], refs[3]
    feats_ref, first_ref, fresh_ref = held
    copies = [pltpu.make_async_copy(s, h, sem.at[i]) for i, (s, h) in enumerate(zip(sources, held))]
    for copy in copies:
        copy.start()
    rows, half = left_ref.shape
    mixed = times_adj(high_ref, low_ref, rows, stacked(came))
    copies[0].wait()
    mixed = mixed + times_adj(high_ref, low_ref, 0, feats_ref[...])
    copies[1].wait()
    mixed = mixed + 0.1 * first_ref[...]
    beta = beta_ref[0]
    out_ref[...] = (1.0 - beta) * mixed + beta * dot3(halves(mixed), halves(weight_ref[...]))
    copies[2].wait()
    last = last_ref[0] != 0
    left_ref[...] = jnp.where(last, fresh_ref[:, :half], first_ref[:, :half])
    right_ref[...] = jnp.where(last, fresh_ref[:, half:], first_ref[:, half:])


def early(beta, last, adj, weight, came, feats, first, fresh):
    rows, width = feats.shape
    arrays = (feats, first, fresh)
    return call(
        early_kernel,
        (beta, last, *adj, weight, *came, *[in_hbm(v) for v in arrays]),
        [SMEM] * 2 + [VMEM] * (3 + len(came)) + [HBM] * 3,
        (vmem(rows, width),) + (vmem(rows, width // 2),) * 2,
        flops=6 * rows * width * (width + rows + len(came) * BLK),
        nbytes=4 * (width * width + 5 * rows * width),
        scratch=[pltpu.VMEM(v.shape, F32) for v in arrays] + [ONE((len(arrays),))],
    )


def late_kernel(beta_ref, last_ref, index_ref, *refs, kinds):
    count = len(kinds)
    got, refs = refs[:count], refs[count:]
    (high_ref, low_ref, base_ref, weight_ref, first_left_ref, first_right_ref, came_ref), refs = refs[:7], refs[7:]
    out_left_ref, out_right_ref, left_ref, right_ref, sent = refs[0], refs[1], refs[2], refs[3], refs[4:]
    half = left_ref.shape[1]
    beta = beta_ref[0]
    last = last_ref[0] != 0
    came = came_ref[...]
    pair = halves(came)
    column = high_ref.shape[1] - BLK
    for at, out_ref, first_ref, next_ref in (
        (half, out_right_ref, first_right_ref, right_ref),
        (0, out_left_ref, first_left_ref, left_ref),
    ):
        cut = slice(at, at + half)
        through = (1.0 - beta) * came[:, cut] + beta * dot3(pair, halves(weight_ref[:, cut]))
        value = jnp.maximum(base_ref[:, cut] + times_adj(high_ref, low_ref, column, through), 0.0)
        out_ref[...] = value
        next_ref[...] = jnp.where(last, first_ref[...], value)
    wanted(kinds, index_ref, got, right_ref, sent)


def late(kinds, beta, last, index, got, adj, base, weight, firsts, came, after=()):
    rows, width = base.shape
    half = width // 2
    return call(
        functools.partial(late_kernel, kinds=kinds),
        (beta, last, index, *[got[k] for k in kinds], *adj, base, weight, *firsts, came),
        [SMEM] * (3 + len(kinds)) + [VMEM] * 7,
        (vmem(rows, half),) * 4 + (vmem(BLK, half),) * len(kinds),
        flops=6 * BLK * width * (width + rows),
        nbytes=4 * width * width + 24 * rows * width,
        after=after,
    )


def right_kernel(high_ref, low_ref, feats_ref, first_ref, left_ref, right_ref, out_ref, handed_ref, sem):
    half = left_ref.shape[1]
    copies = [
        pltpu.make_async_copy(left_ref, handed_ref.at[:, :half], sem.at[0]),
        pltpu.make_async_copy(right_ref, handed_ref.at[:, half:], sem.at[1]),
    ]
    for copy in copies:
        copy.start()
    out_ref[...] = times_adj(high_ref, low_ref, 0, feats_ref[...]) + 0.1 * first_ref[...]
    for copy in copies:
        copy.wait()


def own_right(adj, feats, first, left, right):
    rows, half = feats.shape
    return call(
        right_kernel,
        (*adj, feats, first, left, right),
        [VMEM] * 6,
        (vmem(rows, half), pltpu.HBM((rows, 2 * half), F32)),
        flops=6 * rows * rows * half,
        nbytes=28 * rows * half,
        scratch=[ONE((2,))],
    )


def left_kernel(high_ref, low_ref, feats_ref, first_ref, out_ref):
    out_ref[...] = times_adj(high_ref, low_ref, 0, feats_ref[...]) + 0.1 * first_ref[...]


def own_left(adj, feats, first):
    rows, half = feats.shape
    return call(
        left_kernel,
        (*adj, feats, first),
        [VMEM] * 4,
        (vmem(rows, half),),
        flops=6 * rows * rows * half,
        nbytes=12 * rows * half,
    )[0]


def add_kernel(high_ref, low_ref, base_ref, *refs):
    rows = base_ref.shape[0]
    refs[-1][...] = base_ref[...] + times_adj(high_ref, low_ref, rows, stacked(refs[:-1]))


def add_received(adj, base, came, after=()):
    rows, width = base.shape
    return call(
        add_kernel,
        (*adj, base, *came),
        [VMEM] * (3 + len(came)),
        (vmem(rows, width),),
        flops=6 * rows * len(came) * BLK * width,
        nbytes=8 * rows * width,
        after=after,
    )[0]


def second_kernel(beta_ref, high_ref, low_ref, left_ref, right_ref, weight_ref, *refs, tile):
    came, (out_ref, held, sem) = refs[:-3], refs[-3:]
    rows, half = left_ref.shape
    width = weight_ref.shape[1]
    left = left_ref[...] + times_adj(high_ref, low_ref, rows, stacked(came))
    mixed = (left, right_ref[...])
    pair = halves(jnp.concatenate(mixed, axis=1))
    beta = beta_ref[0]
    copies = []
    for i, at in enumerate(range(0, width, tile)):
        cut = slice(at, at + tile)
        own = mixed[at // half][:, at % half : at % half + tile]
        value = (1.0 - beta) * own + beta * dot3(pair, halves(weight_ref[:, cut]))
        held[:, cut] = jnp.maximum(value, 0.0)
        copies.append(pltpu.make_async_copy(held.at[:, cut], out_ref.at[:, cut], sem.at[i]))
        copies[-1].start()
    for copy in copies:
        copy.wait()


def second_layer(beta, adj, left, right, weight, came, tile=256):
    rows, half = left.shape
    width = weight.shape[1]
    return call(
        functools.partial(second_kernel, tile=tile),
        (beta, *adj, left, right, weight, *came),
        [SMEM] + [VMEM] * (5 + len(came)),
        (pltpu.HBM((rows, width), F32),),
        flops=6 * rows * width * (width + len(came) * BLK // 2),
        nbytes=4 * (width * width + 3 * rows * width),
        scratch=[pltpu.VMEM((rows, width), F32), ONE((width // tile,))],
        vmem=16,
    )[0]


def shards(state, initial, fresh, weights, wants, adj_slot, adj_count, adj_vals):
    section = lax.axis_index("segment")
    part = lax.axis_index("graph")
    beta = jnp.log(0.5 / (section.astype(F32) + 1.0) + 1.0).reshape(1)
    last = (section == lax.axis_size("segment") - 1).astype(jnp.int32).reshape(1)
    feats, first, weight = state[0], initial[0], weights[0]
    half = feats.shape[1] // 2
    asks = wants.reshape(wants.shape[1])

    place = []
    for position in range(2 * REACH):
        stride = position // 2 + 1
        low = (part // stride) % 2 == 0
        phase = jnp.where(low, 1 - position % 2, position % 2)
        place.append(jnp.where(phase == 0, SWAPS.index((stride, 0)), SWAPS.index((stride, 1))))
    place = jnp.stack(place).astype(jnp.int32)
    index = []
    for stride, phase in SWAPS:
        low = (part // stride) % 2 == phase
        index.append(jnp.where(low, 2 * stride - 2, 2 * stride - 1))
    index = jnp.stack(index).astype(jnp.int32)

    got = [swap(asks, *kind) for kind in SWAPS]
    final = len(SWAPS) - 1
    others = tuple(range(final))
    every = tuple(range(len(SWAPS)))

    sent = pick(others, index, got, feats, after=got[final:])
    came = [swap(value, *SWAPS[k]) for k, value in enumerate(sent)]
    *adj, sent = prepare(final, place, adj_slot, adj_count, index, got, adj_vals, feats, after=sent[:1])
    crossing = swap(sent, *SWAPS[final])
    known, first_left, first_right = early(beta, last, adj, weight, came, feats, first, fresh)
    handed_left = hand_on(first_left)
    out_left, out_right, left, right, *sent = late(
        every, beta, last, index, got, adj, known, weight, (first_left, first_right), crossing
    )

    left = hand_on(left)
    came = [swap(value, *kind) for value, kind in zip(sent, SWAPS)]
    mixed, first_out = own_right(adj, right, first_right, out_left, out_right)
    sent = choose(every, index, got, left)
    right = hand_on(add_received(adj, mixed, came, after=sent[:1]))
    came = [swap(value, *kind) for value, kind in zip(sent, SWAPS)]
    mixed = own_left(adj, left, handed_left)
    second_out = second_layer(beta, adj, mixed, right, weight, came)
    return first_out[None], second_out[None]


def solution(mesh):
    return jax.shard_map(
        shards,
        mesh=mesh,
        in_specs=(
            P("segment", "graph", None),
            P("segment", "graph", None),
            P("graph", None),
            P("segment", None, None),
            P("graph", None, None),
            P("graph", None),
            P("graph"),
            P("graph", None, None, None),
        ),
        out_specs=(P("segment", "graph", None), P("segment", "graph", None)),
        check_vma=False,
    )
```

```python
import functools

import jax
import jax.numpy as jnp
from jax import lax
from jax.experimental import pallas as pl
from jax.experimental.pallas import tpu as pltpu
from jax.sharding import PartitionSpec as P

BLK = 128
REACH = 2
F32 = jnp.float32
BF16 = jnp.bfloat16
SWAPS = ((1, 0), (2, 0), (2, 1), (1, 1))
VMEM = pl.BlockSpec(memory_space=pltpu.VMEM)
SMEM = pl.BlockSpec(memory_space=pltpu.SMEM)
HBM = pl.BlockSpec(memory_space=pltpu.HBM)
ONE = pltpu.SemaphoreType.DMA


def swap(value, stride, phase):
    peers = lax.axis_size("graph")
    pairs = []
    for low in range(peers - stride):
        if (low // stride) % 2 == phase:
            pairs += [(low, low + stride), (low + stride, low)]
    return lax.ppermute(value, "graph", sorted(pairs))


def hand_on(value):
    peers = lax.axis_size("segment")
    return lax.ppermute(value, "segment", [(i, (i + 1) % peers) for i in range(peers)])


def halves(value):
    high = value.astype(BF16)
    return high, (value - high.astype(F32)).astype(BF16)


def dot3(a, b):
    times = functools.partial(jnp.dot, preferred_element_type=F32)
    return times(a[0], b[0]) + (times(a[0], b[1]) + times(a[1], b[0]))


def call(kernel, args, in_specs, outs, flops=0, nbytes=0, scratch=(), after=(), vmem=16):
    count = len(args)

    def body(*refs):
        kernel(*refs[:count], *refs[count + len(after) :])

    return pl.pallas_call(
        body,
        out_shape=outs,
        in_specs=list(in_specs) + [VMEM] * len(after),
        out_specs=tuple(VMEM if isinstance(out, jax.ShapeDtypeStruct) else HBM for out in outs),
        scratch_shapes=list(scratch),
        cost_estimate=pl.CostEstimate(flops=flops, bytes_accessed=nbytes, transcendentals=0),
        compiler_params=pltpu.CompilerParams(vmem_limit_bytes=vmem * 2**20),
    )(*args, *after)


def vmem(*shape, dtype=F32):
    return jax.ShapeDtypeStruct(shape, dtype)


def prepare_kernel(place_ref, slot_ref, count_ref, index_ref, got_ref, last_ref, *refs, kind):
    (vals_ref, feats_ref, first_ref, fresh_ref), refs = refs[:4], refs[4:]
    high_ref, low_ref, sent_ref, left_ref, right_ref, held, total, sem = refs
    half = left_ref.shape[1]
    for mine, origin in ((last_ref[0] == 0, first_ref), (last_ref[0] != 0, fresh_ref)):

        @pl.when(mine)
        def _():
            pltpu.make_async_copy(origin.at[:, :half], left_ref, sem.at[2]).start()
            pltpu.make_async_copy(origin.at[:, half:], right_ref, sem.at[3]).start()

    copies = [pltpu.make_async_copy(vals_ref, held, sem.at[0])]
    row = pl.multiple_of(got_ref[index_ref[kind]] * BLK, BLK)
    copies.append(pltpu.make_async_copy(feats_ref.at[pl.ds(row, BLK)], sent_ref, sem.at[1]))
    for copy in copies:
        copy.start()
    total[...] = jnp.zeros_like(total)
    blocks, most = held.shape[:2]
    copies[0].wait()
    for b in range(blocks):
        for k in range(most):
            slot = slot_ref[b, k]
            past = jnp.maximum(slot - blocks, 0)
            column = jnp.where(slot < blocks, slot, blocks + place_ref[past])
            scale = jnp.where(k < count_ref[b], 0.9, 0.0).astype(F32)
            where = pl.ds(pl.multiple_of(column * BLK, BLK), BLK)
            total[b * BLK : (b + 1) * BLK, where] += scale * held[b, k]
    high, low = halves(total[...])
    high_ref[...] = high
    low_ref[...] = low
    copies[1].wait()
    pltpu.make_async_copy(first_ref.at[:, :half], left_ref, sem.at[2]).wait()
    pltpu.make_async_copy(first_ref.at[:, half:], right_ref, sem.at[3]).wait()


def in_hbm(value):
    return pltpu.with_memory_space_constraint(value, pltpu.HBM)


def prepare(kind, place, slots, counts, index, got, last, vals, feats, first, fresh, after=()):
    rows, width = feats.shape
    span = rows + 2 * REACH * BLK
    return call(
        functools.partial(prepare_kernel, kind=kind),
        (place, slots, counts, index, got[kind], last, *[in_hbm(v) for v in (vals, feats, first, fresh)]),
        [SMEM] * 6 + [HBM] * 4,
        (vmem(rows, span, dtype=BF16),) * 2 + (vmem(BLK, width),) + (vmem(rows, width // 2),) * 2,
        nbytes=4 * vals.size + 4 * rows * span,
        scratch=[pltpu.VMEM(vals.shape, F32), pltpu.VMEM((rows, span), F32), ONE((4,))],
        after=after,
    )


def pick_kernel(index_ref, *refs, kinds):
    count = len(kinds)
    got, source, outs, sem = refs[:count], refs[count], refs[count + 1 : -1], refs[-1]
    copies = []
    for i, kind in enumerate(kinds):
        row = pl.multiple_of(got[i][index_ref[kind]] * BLK, BLK)
        copies.append(pltpu.make_async_copy(source.at[pl.ds(row, BLK)], outs[i], sem.at[i]))
        copies[-1].start()
    for copy in copies:
        copy.wait()


def pick(kinds, index, got, source, after=()):
    return call(
        functools.partial(pick_kernel, kinds=kinds),
        (index, *[got[k] for k in kinds], in_hbm(source)),
        [SMEM] * (1 + len(kinds)) + [HBM],
        (vmem(BLK, source.shape[1]),) * len(kinds),
        nbytes=8 * BLK * source.shape[1] * len(kinds),
        scratch=[ONE((len(kinds),))],
        after=after,
    )


def wanted(kinds, index_ref, got, source_ref, outs):
    for kind, got_ref, out_ref in zip(kinds, got, outs):
        row = pl.multiple_of(got_ref[index_ref[kind]] * BLK, BLK)
        out_ref[...] = source_ref[pl.ds(row, BLK), :]


def choose_kernel(index_ref, *refs, kinds):
    count = len(kinds)
    wanted(kinds, index_ref, refs[:count], refs[count], refs[count + 1 :])


def choose(kinds, index, got, source, after=()):
    return call(
        functools.partial(choose_kernel, kinds=kinds),
        (index, *[got[k] for k in kinds], source),
        [SMEM] * (1 + len(kinds)) + [VMEM],
        (vmem(BLK, source.shape[1]),) * len(kinds),
        nbytes=8 * len(kinds) * BLK * source.shape[1],
        after=after,
    )


def times_adj(high_ref, low_ref, at, value):
    cut = slice(at, at + value.shape[0])
    return dot3((high_ref[:, cut], low_ref[:, cut]), halves(value))


def stacked(refs):
    return jnp.concatenate([ref[...] for ref in refs], axis=0)


def early_kernel(beta_ref, high_ref, low_ref, weight_ref, *refs):
    came, sources, out_ref, refs = refs[:-6], refs[-6:-4], refs[-4], refs[-3:]
    held, sem = refs[:2], refs[2]
    feats_ref, first_ref = held
    copies = [pltpu.make_async_copy(s, h, sem.at[i]) for i, (s, h) in enumerate(zip(sources, held))]
    for copy in copies:
        copy.start()
    rows = feats_ref.shape[0]
    mixed = times_adj(high_ref, low_ref, rows, stacked(came))
    copies[0].wait()
    mixed = mixed + times_adj(high_ref, low_ref, 0, feats_ref[...])
    copies[1].wait()
    mixed = mixed + 0.1 * first_ref[...]
    beta = beta_ref[0]
    out_ref[...] = (1.0 - beta) * mixed + beta * dot3(halves(mixed), halves(weight_ref[...]))


def early(beta, adj, weight, came, feats, first):
    rows, width = feats.shape
    arrays = (feats, first)
    return call(
        early_kernel,
        (beta, *adj, weight, *came, *[in_hbm(v) for v in arrays]),
        [SMEM] + [VMEM] * (3 + len(came)) + [HBM] * 2,
        (vmem(rows, width),),
        flops=6 * rows * width * (width + rows + len(came) * BLK),
        nbytes=4 * (width * width + 5 * rows * width),
        scratch=[pltpu.VMEM(v.shape, F32) for v in arrays] + [ONE((len(arrays),))],
    )[0]


def late_kernel(beta_ref, last_ref, index_ref, *refs, kinds):
    count = len(kinds)
    got, refs = refs[:count], refs[count:]
    (high_ref, low_ref, base_ref, weight_ref, first_left_ref, first_right_ref, came_ref), refs = refs[:7], refs[7:]
    out_left_ref, out_right_ref, left_ref, right_ref, sent = refs[0], refs[1], refs[2], refs[3], refs[4:]
    half = left_ref.shape[1]
    beta = beta_ref[0]
    last = last_ref[0] != 0
    came = came_ref[...]
    pair = halves(came)
    column = high_ref.shape[1] - BLK
    for at, out_ref, first_ref, next_ref in (
        (half, out_right_ref, first_right_ref, right_ref),
        (0, out_left_ref, first_left_ref, left_ref),
    ):
        cut = slice(at, at + half)
        through = (1.0 - beta) * came[:, cut] + beta * dot3(pair, halves(weight_ref[:, cut]))
        value = jnp.maximum(base_ref[:, cut] + times_adj(high_ref, low_ref, column, through), 0.0)
        out_ref[...] = value
        next_ref[...] = jnp.where(last, first_ref[...], value)
    wanted(kinds, index_ref, got, right_ref, sent)


def late(kinds, beta, last, index, got, adj, base, weight, firsts, came, after=()):
    rows, width = base.shape
    half = width // 2
    return call(
        functools.partial(late_kernel, kinds=kinds),
        (beta, last, index, *[got[k] for k in kinds], *adj, base, weight, *firsts, came),
        [SMEM] * (3 + len(kinds)) + [VMEM] * 7,
        (vmem(rows, half),) * 4 + (vmem(BLK, half),) * len(kinds),
        flops=6 * BLK * width * (width + rows),
        nbytes=4 * width * width + 24 * rows * width,
        after=after,
    )


def right_kernel(high_ref, low_ref, feats_ref, first_ref, left_ref, right_ref, out_ref, handed_ref, sem):
    half = left_ref.shape[1]
    copies = [
        pltpu.make_async_copy(left_ref, handed_ref.at[:, :half], sem.at[0]),
        pltpu.make_async_copy(right_ref, handed_ref.at[:, half:], sem.at[1]),
    ]
    for copy in copies:
        copy.start()
    out_ref[...] = times_adj(high_ref, low_ref, 0, feats_ref[...]) + 0.1 * first_ref[...]
    for copy in copies:
        copy.wait()


def own_right(adj, feats, first, left, right, after=()):
    rows, half = feats.shape
    return call(
        right_kernel,
        (*adj, feats, first, left, right),
        [VMEM] * 6,
        (vmem(rows, half), pltpu.HBM((rows, 2 * half), F32)),
        flops=6 * rows * rows * half,
        nbytes=28 * rows * half,
        scratch=[ONE((2,))],
        after=after,
    )


def left_kernel(high_ref, low_ref, feats_ref, first_ref, out_ref):
    out_ref[...] = times_adj(high_ref, low_ref, 0, feats_ref[...]) + 0.1 * first_ref[...]


def own_left(adj, feats, first):
    rows, half = feats.shape
    return call(
        left_kernel,
        (*adj, feats, first),
        [VMEM] * 4,
        (vmem(rows, half),),
        flops=6 * rows * rows * half,
        nbytes=12 * rows * half,
    )[0]


def add_kernel(high_ref, low_ref, base_ref, *refs):
    rows = base_ref.shape[0]
    refs[-1][...] = base_ref[...] + times_adj(high_ref, low_ref, rows, stacked(refs[:-1]))


def add_received(adj, base, came, after=()):
    rows, width = base.shape
    return call(
        add_kernel,
        (*adj, base, *came),
        [VMEM] * (3 + len(came)),
        (vmem(rows, width),),
        flops=6 * rows * len(came) * BLK * width,
        nbytes=8 * rows * width,
        after=after,
    )[0]


def second_kernel(beta_ref, high_ref, low_ref, left_ref, right_ref, weight_ref, *refs, tile):
    came, (out_ref, held, sem) = refs[:-3], refs[-3:]
    rows, half = left_ref.shape
    width = weight_ref.shape[1]
    left = left_ref[...] + times_adj(high_ref, low_ref, rows, stacked(came))
    mixed = (left, right_ref[...])
    pair = halves(jnp.concatenate(mixed, axis=1))
    beta = beta_ref[0]
    copies = []
    for i, at in enumerate(range(0, width, tile)):
        cut = slice(at, at + tile)
        own = mixed[at // half][:, at % half : at % half + tile]
        value = (1.0 - beta) * own + beta * dot3(pair, halves(weight_ref[:, cut]))
        held[:, cut] = jnp.maximum(value, 0.0)
        copies.append(pltpu.make_async_copy(held.at[:, cut], out_ref.at[:, cut], sem.at[i]))
        copies[-1].start()
    for copy in copies:
        copy.wait()


def second_layer(beta, adj, left, right, weight, came, tile=256):
    rows, half = left.shape
    width = weight.shape[1]
    return call(
        functools.partial(second_kernel, tile=tile),
        (beta, *adj, left, right, weight, *came),
        [SMEM] + [VMEM] * (5 + len(came)),
        (pltpu.HBM((rows, width), F32),),
        flops=6 * rows * width * (width + len(came) * BLK // 2),
        nbytes=4 * (width * width + 3 * rows * width),
        scratch=[pltpu.VMEM((rows, width), F32), ONE((width // tile,))],
        vmem=16,
    )[0]


def shards(state, initial, fresh, weights, wants, adj_slot, adj_count, adj_vals):
    section = lax.axis_index("segment")
    part = lax.axis_index("graph")
    beta = jnp.log(0.5 / (section.astype(F32) + 1.0) + 1.0).reshape(1)
    last = (section == lax.axis_size("segment") - 1).astype(jnp.int32).reshape(1)
    feats, first, weight = state[0], initial[0], weights[0]
    half = feats.shape[1] // 2
    asks = wants.reshape(wants.shape[1])

    place = []
    for position in range(2 * REACH):
        stride = position // 2 + 1
        low = (part // stride) % 2 == 0
        phase = jnp.where(low, 1 - position % 2, position % 2)
        place.append(jnp.where(phase == 0, SWAPS.index((stride, 0)), SWAPS.index((stride, 1))))
    place = jnp.stack(place).astype(jnp.int32)
    index = []
    for stride, phase in SWAPS:
        low = (part // stride) % 2 == phase
        index.append(jnp.where(low, 2 * stride - 2, 2 * stride - 1))
    index = jnp.stack(index).astype(jnp.int32)

    got = [swap(asks, *kind) for kind in SWAPS]
    final = len(SWAPS) - 1
    others = tuple(range(final))
    every = tuple(range(len(SWAPS)))

    sent = pick(others, index, got, feats, after=got[final:])
    came = [swap(value, *SWAPS[k]) for k, value in enumerate(sent)]
    *adj, sent, first_left, first_right = prepare(
        final, place, adj_slot, adj_count, index, got, last, adj_vals, feats, first, fresh, after=sent[:1]
    )
    crossing = swap(sent, *SWAPS[final])
    handed_left = hand_on(first_left)
    known = early(beta, adj, weight, came, feats, first)
    out_left, out_right, left, right, *sent = late(
        every, beta, last, index, got, adj, known, weight, (first_left, first_right), crossing
    )

    left = hand_on(left)
    came = [swap(value, *kind) for value, kind in zip(sent, SWAPS)]
    mixed, first_out = own_right(adj, right, first_right, out_left, out_right, after=(handed_left,))
    sent = choose(every, index, got, left)
    right = hand_on(add_received(adj, mixed, came, after=sent[:1]))
    came = [swap(value, *kind) for value, kind in zip(sent, SWAPS)]
    mixed = own_left(adj, left, handed_left)
    second_out = second_layer(beta, adj, mixed, right, weight, came)
    return first_out[None], second_out[None]


def solution(mesh):
    return jax.shard_map(
        shards,
        mesh=mesh,
        in_specs=(
            P("segment", "graph", None),
            P("segment", "graph", None),
            P("graph", None),
            P("segment", None, None),
            P("graph", None, None),
            P("graph", None),
            P("graph"),
            P("graph", None, None, None),
        ),
        out_specs=(P("segment", "graph", None), P("segment", "graph", None)),
        check_vma=False,
    )
```

```python
import functools

import jax
import jax.numpy as jnp
from jax import lax
from jax.experimental import pallas as pl
from jax.experimental.pallas import tpu as pltpu
from jax.sharding import PartitionSpec as P

BLK = 128
REACH = 2
F32 = jnp.float32
BF16 = jnp.bfloat16
SWAPS = ((1, 0), (2, 0), (2, 1), (1, 1))
VMEM = pl.BlockSpec(memory_space=pltpu.VMEM)
SMEM = pl.BlockSpec(memory_space=pltpu.SMEM)
HBM = pl.BlockSpec(memory_space=pltpu.HBM)
ONE = pltpu.SemaphoreType.DMA


def swap(value, stride, phase):
    peers = lax.axis_size("graph")
    pairs = []
    for low in range(peers - stride):
        if (low // stride) % 2 == phase:
            pairs += [(low, low + stride), (low + stride, low)]
    return lax.ppermute(value, "graph", sorted(pairs))


def hand_on(value):
    peers = lax.axis_size("segment")
    return lax.ppermute(value, "segment", [(i, (i + 1) % peers) for i in range(peers)])


def halves(value):
    high = value.astype(BF16)
    return high, (value - high.astype(F32)).astype(BF16)


def dot3(a, b):
    times = functools.partial(jnp.dot, preferred_element_type=F32)
    return times(a[0], b[0]) + (times(a[0], b[1]) + times(a[1], b[0]))


def call(kernel, args, in_specs, outs, flops=0, nbytes=0, scratch=(), after=(), vmem=16):
    count = len(args)

    def body(*refs):
        kernel(*refs[:count], *refs[count + len(after) :])

    return pl.pallas_call(
        body,
        out_shape=outs,
        in_specs=list(in_specs) + [VMEM] * len(after),
        out_specs=tuple(VMEM if isinstance(out, jax.ShapeDtypeStruct) else HBM for out in outs),
        scratch_shapes=list(scratch),
        cost_estimate=pl.CostEstimate(flops=flops, bytes_accessed=nbytes, transcendentals=0),
        compiler_params=pltpu.CompilerParams(vmem_limit_bytes=vmem * 2**20),
    )(*args, *after)


def vmem(*shape, dtype=F32):
    return jax.ShapeDtypeStruct(shape, dtype)


def prepare_kernel(place_ref, slot_ref, count_ref, index_ref, got_ref, last_ref, *refs, kind):
    (vals_ref, feats_ref, first_ref, fresh_ref), refs = refs[:4], refs[4:]
    high_ref, low_ref, sent_ref, left_ref, right_ref, held, total, sem = refs
    half = left_ref.shape[1]
    for mine, origin in ((last_ref[0] == 0, first_ref), (last_ref[0] != 0, fresh_ref)):

        @pl.when(mine)
        def _():
            pltpu.make_async_copy(origin.at[:, :half], left_ref, sem.at[2]).start()
            pltpu.make_async_copy(origin.at[:, half:], right_ref, sem.at[3]).start()

    copies = [pltpu.make_async_copy(vals_ref, held, sem.at[0])]
    row = pl.multiple_of(got_ref[index_ref[kind]] * BLK, BLK)
    copies.append(pltpu.make_async_copy(feats_ref.at[pl.ds(row, BLK)], sent_ref, sem.at[1]))
    for copy in copies:
        copy.start()
    total[...] = jnp.zeros_like(total)
    blocks, most = held.shape[:2]
    copies[0].wait()
    for b in range(blocks):
        for k in range(most):
            slot = slot_ref[b, k]
            past = jnp.maximum(slot - blocks, 0)
            column = jnp.where(slot < blocks, slot, blocks + place_ref[past])
            scale = jnp.where(k < count_ref[b], 0.9, 0.0).astype(F32)
            where = pl.ds(pl.multiple_of(column * BLK, BLK), BLK)
            total[b * BLK : (b + 1) * BLK, where] += scale * held[b, k]
    high, low = halves(total[...])
    high_ref[...] = high
    low_ref[...] = low
    copies[1].wait()
    pltpu.make_async_copy(first_ref.at[:, :half], left_ref, sem.at[2]).wait()
    pltpu.make_async_copy(first_ref.at[:, half:], right_ref, sem.at[3]).wait()


def in_hbm(value):
    return pltpu.with_memory_space_constraint(value, pltpu.HBM)


def prepare(kind, place, slots, counts, index, got, last, vals, feats, first, fresh, after=()):
    rows, width = feats.shape
    span = rows + 2 * REACH * BLK
    return call(
        functools.partial(prepare_kernel, kind=kind),
        (place, slots, counts, index, got[kind], last, *[in_hbm(v) for v in (vals, feats, first, fresh)]),
        [SMEM] * 6 + [HBM] * 4,
        (vmem(rows, span, dtype=BF16),) * 2 + (vmem(BLK, width),) + (vmem(rows, width // 2),) * 2,
        nbytes=4 * vals.size + 4 * rows * span,
        scratch=[pltpu.VMEM(vals.shape, F32), pltpu.VMEM((rows, span), F32), ONE((4,))],
        after=after,
    )


def pick_kernel(index_ref, *refs, kinds):
    count = len(kinds)
    got, source, outs, sem = refs[:count], refs[count], refs[count + 1 : -1], refs[-1]
    copies = []
    for i, kind in enumerate(kinds):
        row = pl.multiple_of(got[i][index_ref[kind]] * BLK, BLK)
        copies.append(pltpu.make_async_copy(source.at[pl.ds(row, BLK)], outs[i], sem.at[i]))
        copies[-1].start()
    for copy in copies:
        copy.wait()


def pick(kinds, index, got, source, after=()):
    return call(
        functools.partial(pick_kernel, kinds=kinds),
        (index, *[got[k] for k in kinds], in_hbm(source)),
        [SMEM] * (1 + len(kinds)) + [HBM],
        (vmem(BLK, source.shape[1]),) * len(kinds),
        nbytes=8 * BLK * source.shape[1] * len(kinds),
        scratch=[ONE((len(kinds),))],
        after=after,
    )


def wanted(kinds, index_ref, got, source_ref, outs):
    for kind, got_ref, out_ref in zip(kinds, got, outs):
        row = pl.multiple_of(got_ref[index_ref[kind]] * BLK, BLK)
        out_ref[...] = source_ref[pl.ds(row, BLK), :]


def choose_kernel(index_ref, *refs, kinds):
    count = len(kinds)
    wanted(kinds, index_ref, refs[:count], refs[count], refs[count + 1 :])


def choose(kinds, index, got, source, after=()):
    return call(
        functools.partial(choose_kernel, kinds=kinds),
        (index, *[got[k] for k in kinds], source),
        [SMEM] * (1 + len(kinds)) + [VMEM],
        (vmem(BLK, source.shape[1]),) * len(kinds),
        nbytes=8 * len(kinds) * BLK * source.shape[1],
        after=after,
    )


def times_adj(high_ref, low_ref, at, value):
    cut = slice(at, at + value.shape[0])
    return dot3((high_ref[:, cut], low_ref[:, cut]), halves(value))


def stacked(refs):
    return jnp.concatenate([ref[...] for ref in refs], axis=0)


def mix_kernel(high_ref, low_ref, *refs):
    sources, out_ref, held, sem = refs[:2], refs[2], refs[3:5], refs[5]
    copies = [pltpu.make_async_copy(s, h, sem.at[i]) for i, (s, h) in enumerate(zip(sources, held))]
    for copy in copies:
        copy.start()
    for copy in copies:
        copy.wait()
    out_ref[...] = times_adj(high_ref, low_ref, 0, held[0][...]) + 0.1 * held[1][...]


def own_first(adj, feats, first):
    rows, width = feats.shape
    return call(
        mix_kernel,
        (*adj, in_hbm(feats), in_hbm(first)),
        [VMEM] * 2 + [HBM] * 2,
        (vmem(rows, width),),
        flops=6 * rows * rows * width,
        nbytes=12 * rows * width,
        scratch=[pltpu.VMEM(feats.shape, F32)] * 2 + [ONE((2,))],
    )[0]


def early_kernel(beta_ref, high_ref, low_ref, weight_ref, base_ref, *refs):
    came, out_ref = refs[:-1], refs[-1]
    rows = base_ref.shape[0]
    mixed = base_ref[...] + times_adj(high_ref, low_ref, rows, stacked(came))
    beta = beta_ref[0]
    out_ref[...] = (1.0 - beta) * mixed + beta * dot3(halves(mixed), halves(weight_ref[...]))


def early(beta, adj, weight, base, came):
    rows, width = base.shape
    return call(
        early_kernel,
        (beta, *adj, weight, base, *came),
        [SMEM] + [VMEM] * (4 + len(came)),
        (vmem(rows, width),),
        flops=6 * rows * width * (width + len(came) * BLK),
        nbytes=4 * (width * width + 2 * rows * width),
    )[0]


def late_kernel(beta_ref, last_ref, index_ref, *refs, kinds):
    count = len(kinds)
    got, refs = refs[:count], refs[count:]
    (high_ref, low_ref, base_ref, weight_ref, first_left_ref, first_right_ref, came_ref), refs = refs[:7], refs[7:]
    out_left_ref, out_right_ref, left_ref, right_ref, sent = refs[0], refs[1], refs[2], refs[3], refs[4:]
    half = left_ref.shape[1]
    beta = beta_ref[0]
    last = last_ref[0] != 0
    came = came_ref[...]
    pair = halves(came)
    column = high_ref.shape[1] - BLK
    for at, out_ref, first_ref, next_ref in (
        (half, out_right_ref, first_right_ref, right_ref),
        (0, out_left_ref, first_left_ref, left_ref),
    ):
        cut = slice(at, at + half)
        through = (1.0 - beta) * came[:, cut] + beta * dot3(pair, halves(weight_ref[:, cut]))
        value = jnp.maximum(base_ref[:, cut] + times_adj(high_ref, low_ref, column, through), 0.0)
        out_ref[...] = value
        next_ref[...] = jnp.where(last, first_ref[...], value)
    wanted(kinds, index_ref, got, right_ref, sent)


def late(kinds, beta, last, index, got, adj, base, weight, firsts, came, after=()):
    rows, width = base.shape
    half = width // 2
    return call(
        functools.partial(late_kernel, kinds=kinds),
        (beta, last, index, *[got[k] for k in kinds], *adj, base, weight, *firsts, came),
        [SMEM] * (3 + len(kinds)) + [VMEM] * 7,
        (vmem(rows, half),) * 4 + (vmem(BLK, half),) * len(kinds),
        flops=6 * BLK * width * (width + rows),
        nbytes=4 * width * width + 24 * rows * width,
        after=after,
    )


def right_kernel(high_ref, low_ref, feats_ref, first_ref, left_ref, right_ref, out_ref, handed_ref, sem):
    half = left_ref.shape[1]
    copies = [
        pltpu.make_async_copy(left_ref, handed_ref.at[:, :half], sem.at[0]),
        pltpu.make_async_copy(right_ref, handed_ref.at[:, half:], sem.at[1]),
    ]
    for copy in copies:
        copy.start()
    out_ref[...] = times_adj(high_ref, low_ref, 0, feats_ref[...]) + 0.1 * first_ref[...]
    for copy in copies:
        copy.wait()


def own_right(adj, feats, first, left, right, after=()):
    rows, half = feats.shape
    return call(
        right_kernel,
        (*adj, feats, first, left, right),
        [VMEM] * 6,
        (vmem(rows, half), pltpu.HBM((rows, 2 * half), F32)),
        flops=6 * rows * rows * half,
        nbytes=28 * rows * half,
        scratch=[ONE((2,))],
        after=after,
    )


def left_kernel(high_ref, low_ref, feats_ref, first_ref, out_ref):
    out_ref[...] = times_adj(high_ref, low_ref, 0, feats_ref[...]) + 0.1 * first_ref[...]


def own_left(adj, feats, first):
    rows, half = feats.shape
    return call(
        left_kernel,
        (*adj, feats, first),
        [VMEM] * 4,
        (vmem(rows, half),),
        flops=6 * rows * rows * half,
        nbytes=12 * rows * half,
    )[0]


def add_kernel(high_ref, low_ref, base_ref, *refs):
    rows = base_ref.shape[0]
    refs[-1][...] = base_ref[...] + times_adj(high_ref, low_ref, rows, stacked(refs[:-1]))


def add_received(adj, base, came, after=()):
    rows, width = base.shape
    return call(
        add_kernel,
        (*adj, base, *came),
        [VMEM] * (3 + len(came)),
        (vmem(rows, width),),
        flops=6 * rows * len(came) * BLK * width,
        nbytes=8 * rows * width,
        after=after,
    )[0]


def term_kernel(beta_ref, right_ref, weight_ref, out_ref):
    half = right_ref.shape[1]
    right = right_ref[...]
    beta = beta_ref[0]
    term = beta * dot3(halves(right), halves(weight_ref[half:, :]))
    out_ref[:, :half] = term[:, :half]
    out_ref[:, half:] = term[:, half:] + (1.0 - beta) * right


def right_term(beta, right, weight):
    rows, half = right.shape
    width = weight.shape[1]
    return call(
        term_kernel,
        (beta, right, weight),
        [SMEM] + [VMEM] * 2,
        (vmem(rows, width),),
        flops=6 * rows * half * width,
        nbytes=4 * (half * width + 2 * rows * width),
    )[0]


def second_kernel(beta_ref, high_ref, low_ref, left_ref, term_ref, weight_ref, *refs, tile):
    came, (out_ref, held, sem) = refs[:-3], refs[-3:]
    rows, half = left_ref.shape
    width = weight_ref.shape[1]
    left = left_ref[...] + times_adj(high_ref, low_ref, rows, stacked(came))
    pair = halves(left)
    beta = beta_ref[0]
    copies = []
    for i, at in enumerate(range(0, width, tile)):
        cut = slice(at, at + tile)
        value = term_ref[:, cut] + beta * dot3(pair, halves(weight_ref[:half, cut]))
        if at < half:
            value = value + (1.0 - beta) * left[:, cut]
        held[:, cut] = jnp.maximum(value, 0.0)
        copies.append(pltpu.make_async_copy(held.at[:, cut], out_ref.at[:, cut], sem.at[i]))
        copies[-1].start()
    for copy in copies:
        copy.wait()


def second_layer(beta, adj, left, term, weight, came, tile=256):
    rows, half = left.shape
    width = weight.shape[1]
    return call(
        functools.partial(second_kernel, tile=tile),
        (beta, *adj, left, term, weight, *came),
        [SMEM] + [VMEM] * (5 + len(came)),
        (pltpu.HBM((rows, width), F32),),
        flops=6 * rows * half * (width + len(came) * BLK),
        nbytes=4 * (half * width + 3 * rows * width),
        scratch=[pltpu.VMEM((rows, width), F32), ONE((width // tile,))],
    )[0]


def shards(state, initial, fresh, weights, wants, adj_slot, adj_count, adj_vals):
    section = lax.axis_index("segment")
    part = lax.axis_index("graph")
    beta = jnp.log(0.5 / (section.astype(F32) + 1.0) + 1.0).reshape(1)
    last = (section == lax.axis_size("segment") - 1).astype(jnp.int32).reshape(1)
    feats, first, weight = state[0], initial[0], weights[0]
    half = feats.shape[1] // 2
    asks = wants.reshape(wants.shape[1])

    place = []
    for position in range(2 * REACH):
        stride = position // 2 + 1
        low = (part // stride) % 2 == 0
        phase = jnp.where(low, 1 - position % 2, position % 2)
        place.append(jnp.where(phase == 0, SWAPS.index((stride, 0)), SWAPS.index((stride, 1))))
    place = jnp.stack(place).astype(jnp.int32)
    index = []
    for stride, phase in SWAPS:
        low = (part // stride) % 2 == phase
        index.append(jnp.where(low, 2 * stride - 2, 2 * stride - 1))
    index = jnp.stack(index).astype(jnp.int32)

    got = [swap(asks, *kind) for kind in SWAPS]
    final = len(SWAPS) - 1
    others = tuple(range(final))
    every = tuple(range(len(SWAPS)))

    sent = pick(others, index, got, feats, after=got[final:])
    came = [swap(value, *SWAPS[k]) for k, value in enumerate(sent)]
    *adj, sent, first_left, first_right = prepare(
        final, place, adj_slot, adj_count, index, got, last, adj_vals, feats, first, fresh, after=sent[:1]
    )
    crossing = swap(sent, *SWAPS[final])
    handed_left = hand_on(first_left)
    known = early(beta, adj, weight, own_first(adj, feats, first), came)
    out_left, out_right, left, right, *sent = late(
        every, beta, last, index, got, adj, known, weight, (first_left, first_right), crossing
    )

    left = hand_on(left)
    came = [swap(value, *kind) for value, kind in zip(sent, SWAPS)]
    mixed, first_out = own_right(adj, right, first_right, out_left, out_right, after=(handed_left,))
    sent = choose(every, index, got, left)
    right = hand_on(add_received(adj, mixed, came, after=sent[:1]))
    came = [swap(value, *kind) for value, kind in zip(sent, SWAPS)]
    mixed = own_left(adj, left, handed_left)
    second_out = second_layer(beta, adj, mixed, right_term(beta, right, weight), weight, came)
    return first_out[None], second_out[None]


def solution(mesh):
    return jax.shard_map(
        shards,
        mesh=mesh,
        in_specs=(
            P("segment", "graph", None),
            P("segment", "graph", None),
            P("graph", None),
            P("segment", None, None),
            P("graph", None, None),
            P("graph", None),
            P("graph"),
            P("graph", None, None, None),
        ),
        out_specs=(P("segment", "graph", None), P("segment", "graph", None)),
        check_vma=False,
    )
```

```python
import functools

import jax
import jax.numpy as jnp
from jax import lax
from jax.experimental import pallas as pl
from jax.experimental.pallas import tpu as pltpu
from jax.sharding import PartitionSpec as P

BLK = 128
REACH = 2
F32 = jnp.float32
BF16 = jnp.bfloat16
SWAPS = ((1, 0), (2, 0), (2, 1), (1, 1))
VMEM = pl.BlockSpec(memory_space=pltpu.VMEM)
SMEM = pl.BlockSpec(memory_space=pltpu.SMEM)
HBM = pl.BlockSpec(memory_space=pltpu.HBM)
ONE = pltpu.SemaphoreType.DMA


def swap(value, stride, phase):
    peers = lax.axis_size("graph")
    pairs = []
    for low in range(peers - stride):
        if (low // stride) % 2 == phase:
            pairs += [(low, low + stride), (low + stride, low)]
    return lax.ppermute(value, "graph", sorted(pairs))


def hand_on(value):
    peers = lax.axis_size("segment")
    return lax.ppermute(value, "segment", [(i, (i + 1) % peers) for i in range(peers)])


def halves(value):
    high = value.astype(BF16)
    return high, (value - high.astype(F32)).astype(BF16)


def dot3(a, b):
    times = functools.partial(jnp.dot, preferred_element_type=F32)
    return times(a[0], b[0]) + (times(a[0], b[1]) + times(a[1], b[0]))


def call(kernel, args, in_specs, outs, flops=0, nbytes=0, scratch=(), after=(), vmem=16):
    count = len(args)

    def body(*refs):
        kernel(*refs[:count], *refs[count + len(after) :])

    return pl.pallas_call(
        body,
        out_shape=outs,
        in_specs=list(in_specs) + [VMEM] * len(after),
        out_specs=tuple(VMEM if isinstance(out, jax.ShapeDtypeStruct) else HBM for out in outs),
        scratch_shapes=list(scratch),
        cost_estimate=pl.CostEstimate(flops=flops, bytes_accessed=nbytes, transcendentals=0),
        compiler_params=pltpu.CompilerParams(vmem_limit_bytes=vmem * 2**20),
    )(*args, *after)


def vmem(*shape, dtype=F32):
    return jax.ShapeDtypeStruct(shape, dtype)


def prepare_kernel(place_ref, slot_ref, count_ref, index_ref, got_ref, last_ref, *refs, kind):
    (vals_ref, feats_ref, first_ref, fresh_ref), refs = refs[:4], refs[4:]
    high_ref, low_ref, sent_ref, left_ref, right_ref, held, total, sem = refs
    half = left_ref.shape[1]
    for mine, origin in ((last_ref[0] == 0, first_ref), (last_ref[0] != 0, fresh_ref)):

        @pl.when(mine)
        def _():
            pltpu.make_async_copy(origin.at[:, :half], left_ref, sem.at[2]).start()
            pltpu.make_async_copy(origin.at[:, half:], right_ref, sem.at[3]).start()

    copies = [pltpu.make_async_copy(vals_ref, held, sem.at[0])]
    row = pl.multiple_of(got_ref[index_ref[kind]] * BLK, BLK)
    copies.append(pltpu.make_async_copy(feats_ref.at[pl.ds(row, BLK)], sent_ref, sem.at[1]))
    for copy in copies:
        copy.start()
    total[...] = jnp.zeros_like(total)
    blocks, most = held.shape[:2]
    copies[0].wait()
    for b in range(blocks):
        for k in range(most):
            slot = slot_ref[b, k]
            past = jnp.maximum(slot - blocks, 0)
            column = jnp.where(slot < blocks, slot, blocks + place_ref[past])
            scale = jnp.where(k < count_ref[b], 0.9, 0.0).astype(F32)
            where = pl.ds(pl.multiple_of(column * BLK, BLK), BLK)
            total[b * BLK : (b + 1) * BLK, where] += scale * held[b, k]
    high, low = halves(total[...])
    high_ref[...] = high
    low_ref[...] = low
    copies[1].wait()
    pltpu.make_async_copy(first_ref.at[:, :half], left_ref, sem.at[2]).wait()
    pltpu.make_async_copy(first_ref.at[:, half:], right_ref, sem.at[3]).wait()


def in_hbm(value):
    return pltpu.with_memory_space_constraint(value, pltpu.HBM)


def prepare(kind, place, slots, counts, index, got, last, vals, feats, first, fresh, after=()):
    rows, width = feats.shape
    span = rows + 2 * REACH * BLK
    return call(
        functools.partial(prepare_kernel, kind=kind),
        (place, slots, counts, index, got[kind], last, *[in_hbm(v) for v in (vals, feats, first, fresh)]),
        [SMEM] * 6 + [HBM] * 4,
        (vmem(rows, span, dtype=BF16),) * 2 + (vmem(BLK, width),) + (vmem(rows, width // 2),) * 2,
        nbytes=4 * vals.size + 4 * rows * span,
        scratch=[pltpu.VMEM(vals.shape, F32), pltpu.VMEM((rows, span), F32), ONE((4,))],
        after=after,
    )


def pick_kernel(index_ref, *refs, kinds):
    count = len(kinds)
    got, source, outs, sem = refs[:count], refs[count], refs[count + 1 : -1], refs[-1]
    copies = []
    for i, kind in enumerate(kinds):
        row = pl.multiple_of(got[i][index_ref[kind]] * BLK, BLK)
        copies.append(pltpu.make_async_copy(source.at[pl.ds(row, BLK)], outs[i], sem.at[i]))
        copies[-1].start()
    for copy in copies:
        copy.wait()


def pick(kinds, index, got, source, after=()):
    return call(
        functools.partial(pick_kernel, kinds=kinds),
        (index, *[got[k] for k in kinds], in_hbm(source)),
        [SMEM] * (1 + len(kinds)) + [HBM],
        (vmem(BLK, source.shape[1]),) * len(kinds),
        nbytes=8 * BLK * source.shape[1] * len(kinds),
        scratch=[ONE((len(kinds),))],
        after=after,
    )


def wanted(kinds, index_ref, got, source_ref, outs):
    for kind, got_ref, out_ref in zip(kinds, got, outs):
        row = pl.multiple_of(got_ref[index_ref[kind]] * BLK, BLK)
        out_ref[...] = source_ref[pl.ds(row, BLK), :]


def choose_kernel(index_ref, *refs, kinds):
    count = len(kinds)
    wanted(kinds, index_ref, refs[:count], refs[count], refs[count + 1 :])


def choose(kinds, index, got, source, after=()):
    return call(
        functools.partial(choose_kernel, kinds=kinds),
        (index, *[got[k] for k in kinds], source),
        [SMEM] * (1 + len(kinds)) + [VMEM],
        (vmem(BLK, source.shape[1]),) * len(kinds),
        nbytes=8 * len(kinds) * BLK * source.shape[1],
        after=after,
    )


def times_adj(high_ref, low_ref, at, value):
    cut = slice(at, at + value.shape[0])
    a, b = (high_ref[:, cut], low_ref[:, cut]), halves(value)
    rows, columns = jnp.concatenate([a[0], a[1], a[0]], axis=1), jnp.concatenate([b[0], b[0], b[1]], axis=0)
    return jnp.dot(rows, columns, preferred_element_type=F32)


def stacked(refs):
    return jnp.concatenate([ref[...] for ref in refs], axis=0)


def mix_kernel(high_ref, low_ref, *refs):
    sources, out_ref, held, sem = refs[:2], refs[2], refs[3:5], refs[5]
    copies = [pltpu.make_async_copy(s, h, sem.at[i]) for i, (s, h) in enumerate(zip(sources, held))]
    for copy in copies:
        copy.start()
    for copy in copies:
        copy.wait()
    out_ref[...] = times_adj(high_ref, low_ref, 0, held[0][...]) + 0.1 * held[1][...]


def own_first(adj, feats, first):
    rows, width = feats.shape
    return call(
        mix_kernel,
        (*adj, in_hbm(feats), in_hbm(first)),
        [VMEM] * 2 + [HBM] * 2,
        (vmem(rows, width),),
        flops=6 * rows * rows * width,
        nbytes=12 * rows * width,
        scratch=[pltpu.VMEM(feats.shape, F32)] * 2 + [ONE((2,))],
    )[0]


def early_kernel(beta_ref, high_ref, low_ref, weight_ref, base_ref, *refs):
    came, out_ref = refs[:-1], refs[-1]
    rows = base_ref.shape[0]
    mixed = base_ref[...] + times_adj(high_ref, low_ref, rows, stacked(came))
    beta = beta_ref[0]
    out_ref[...] = (1.0 - beta) * mixed + beta * dot3(halves(mixed), halves(weight_ref[...]))


def early(beta, adj, weight, base, came):
    rows, width = base.shape
    return call(
        early_kernel,
        (beta, *adj, weight, base, *came),
        [SMEM] + [VMEM] * (4 + len(came)),
        (vmem(rows, width),),
        flops=6 * rows * width * (width + len(came) * BLK),
        nbytes=4 * (width * width + 2 * rows * width),
    )[0]


def late_kernel(beta_ref, last_ref, index_ref, *refs, kinds):
    count = len(kinds)
    got, refs = refs[:count], refs[count:]
    (high_ref, low_ref, base_ref, weight_ref, first_left_ref, first_right_ref, came_ref), refs = refs[:7], refs[7:]
    out_left_ref, out_right_ref, left_ref, right_ref, sent = refs[0], refs[1], refs[2], refs[3], refs[4:]
    half = left_ref.shape[1]
    beta = beta_ref[0]
    last = last_ref[0] != 0
    came = came_ref[...]
    pair = halves(came)
    column = high_ref.shape[1] - BLK
    for at, out_ref, first_ref, next_ref in (
        (half, out_right_ref, first_right_ref, right_ref),
        (0, out_left_ref, first_left_ref, left_ref),
    ):
        cut = slice(at, at + half)
        through = (1.0 - beta) * came[:, cut] + beta * dot3(pair, halves(weight_ref[:, cut]))
        value = jnp.maximum(base_ref[:, cut] + times_adj(high_ref, low_ref, column, through), 0.0)
        out_ref[...] = value
        next_ref[...] = jnp.where(last, first_ref[...], value)
    wanted(kinds, index_ref, got, right_ref, sent)


def late(kinds, beta, last, index, got, adj, base, weight, firsts, came, after=()):
    rows, width = base.shape
    half = width // 2
    return call(
        functools.partial(late_kernel, kinds=kinds),
        (beta, last, index, *[got[k] for k in kinds], *adj, base, weight, *firsts, came),
        [SMEM] * (3 + len(kinds)) + [VMEM] * 7,
        (vmem(rows, half),) * 4 + (vmem(BLK, half),) * len(kinds),
        flops=6 * BLK * width * (width + rows),
        nbytes=4 * width * width + 24 * rows * width,
        after=after,
    )


def right_kernel(high_ref, low_ref, feats_ref, first_ref, left_ref, right_ref, out_ref, handed_ref, sem):
    half = left_ref.shape[1]
    copies = [
        pltpu.make_async_copy(left_ref, handed_ref.at[:, :half], sem.at[0]),
        pltpu.make_async_copy(right_ref, handed_ref.at[:, half:], sem.at[1]),
    ]
    for copy in copies:
        copy.start()
    out_ref[...] = times_adj(high_ref, low_ref, 0, feats_ref[...]) + 0.1 * first_ref[...]
    for copy in copies:
        copy.wait()


def own_right(adj, feats, first, left, right, after=()):
    rows, half = feats.shape
    return call(
        right_kernel,
        (*adj, feats, first, left, right),
        [VMEM] * 6,
        (vmem(rows, half), pltpu.HBM((rows, 2 * half), F32)),
        flops=6 * rows * rows * half,
        nbytes=28 * rows * half,
        scratch=[ONE((2,))],
        after=after,
    )


def left_kernel(high_ref, low_ref, feats_ref, first_ref, *refs):
    came, out_ref = refs[:-1], refs[-1]
    out_ref[...] = times_adj(high_ref, low_ref, 0, stacked((feats_ref, *came))) + 0.1 * first_ref[...]


def own_left(adj, feats, first, came):
    rows, half = feats.shape
    return call(
        left_kernel,
        (*adj, feats, first, *came),
        [VMEM] * (4 + len(came)),
        (vmem(rows, half),),
        flops=6 * rows * rows * half,
        nbytes=12 * rows * half,
    )[0]


def add_kernel(high_ref, low_ref, base_ref, *refs):
    rows = base_ref.shape[0]
    refs[-1][...] = base_ref[...] + times_adj(high_ref, low_ref, rows, stacked(refs[:-1]))


def add_received(adj, base, came, after=()):
    rows, width = base.shape
    return call(
        add_kernel,
        (*adj, base, *came),
        [VMEM] * (3 + len(came)),
        (vmem(rows, width),),
        flops=6 * rows * len(came) * BLK * width,
        nbytes=8 * rows * width,
        after=after,
    )[0]


def term_kernel(beta_ref, right_ref, weight_ref, out_ref):
    half = right_ref.shape[1]
    right = right_ref[...]
    beta = beta_ref[0]
    term = beta * dot3(halves(right), halves(weight_ref[half:, :]))
    out_ref[:, :half] = term[:, :half]
    out_ref[:, half:] = term[:, half:] + (1.0 - beta) * right


def right_term(beta, right, weight):
    rows, half = right.shape
    width = weight.shape[1]
    return call(
        term_kernel,
        (beta, right, weight),
        [SMEM] + [VMEM] * 2,
        (vmem(rows, width),),
        flops=6 * rows * half * width,
        nbytes=4 * (half * width + 2 * rows * width),
    )[0]


def known_kernel(beta_ref, high_ref, low_ref, left_ref, term_ref, weight_ref, *refs):
    came, out_ref = refs[:-1], refs[-1]
    rows, half = left_ref.shape
    column = high_ref.shape[1] - BLK - len(came) * BLK
    left = left_ref[...] + times_adj(high_ref, low_ref, column, stacked(came))
    beta = beta_ref[0]
    value = term_ref[...] + beta * dot3(halves(left), halves(weight_ref[:half, :]))
    out_ref[:, :half] = value[:, :half] + (1.0 - beta) * left
    out_ref[:, half:] = value[:, half:]


def second_known(beta, adj, left, term, weight, came):
    rows, half = left.shape
    width = weight.shape[1]
    return call(
        known_kernel,
        (beta, *adj, left, term, weight, *came),
        [SMEM] + [VMEM] * (5 + len(came)),
        (vmem(rows, width),),
        flops=6 * rows * half * (width + len(came) * BLK),
        nbytes=4 * (half * width + 3 * rows * width),
    )[0]


def second_kernel(beta_ref, high_ref, low_ref, base_ref, weight_ref, came_ref, out_ref, held, sem, *, tile):
    half = came_ref.shape[1]
    width = weight_ref.shape[1]
    came = came_ref[...]
    pair = halves(came)
    beta = beta_ref[0]
    column = high_ref.shape[1] - BLK
    copies = []
    for i, at in enumerate(range(0, width, tile)):
        cut = slice(at, at + tile)
        through = beta * dot3(pair, halves(weight_ref[:half, cut]))
        if at < half:
            through = through + (1.0 - beta) * came[:, cut]
        held[:, cut] = jnp.maximum(base_ref[:, cut] + times_adj(high_ref, low_ref, column, through), 0.0)
        copies.append(pltpu.make_async_copy(held.at[:, cut], out_ref.at[:, cut], sem.at[i]))
        copies[-1].start()
    for copy in copies:
        copy.wait()


def second_layer(beta, adj, base, weight, came, tile=256):
    rows, width = base.shape
    half = came.shape[1]
    return call(
        functools.partial(second_kernel, tile=tile),
        (beta, *adj, base, weight, came),
        [SMEM] + [VMEM] * 5,
        (pltpu.HBM((rows, width), F32),),
        flops=6 * BLK * width * (half + rows),
        nbytes=4 * (half * width + 3 * rows * width),
        scratch=[pltpu.VMEM((rows, width), F32), ONE((width // tile,))],
    )[0]


def shards(state, initial, fresh, weights, wants, adj_slot, adj_count, adj_vals):
    section = lax.axis_index("segment")
    part = lax.axis_index("graph")
    beta = jnp.log(0.5 / (section.astype(F32) + 1.0) + 1.0).reshape(1)
    last = (section == lax.axis_size("segment") - 1).astype(jnp.int32).reshape(1)
    feats, first, weight = state[0], initial[0], weights[0]
    half = feats.shape[1] // 2
    asks = wants.reshape(wants.shape[1])

    place = []
    for position in range(2 * REACH):
        stride = position // 2 + 1
        low = (part // stride) % 2 == 0
        phase = jnp.where(low, 1 - position % 2, position % 2)
        place.append(jnp.where(phase == 0, SWAPS.index((stride, 0)), SWAPS.index((stride, 1))))
    place = jnp.stack(place).astype(jnp.int32)
    index = []
    for stride, phase in SWAPS:
        low = (part // stride) % 2 == phase
        index.append(jnp.where(low, 2 * stride - 2, 2 * stride - 1))
    index = jnp.stack(index).astype(jnp.int32)

    got = [swap(asks, *kind) for kind in SWAPS]
    final = len(SWAPS) - 1
    others = tuple(range(final))
    every = tuple(range(len(SWAPS)))

    sent = pick(others, index, got, feats, after=got[final:])
    came = [swap(value, *SWAPS[k]) for k, value in enumerate(sent)]
    *adj, sent, first_left, first_right = prepare(
        final, place, adj_slot, adj_count, index, got, last, adj_vals, feats, first, fresh, after=sent[:1]
    )
    crossing = swap(sent, *SWAPS[final])
    handed_left = hand_on(first_left)
    known = early(beta, adj, weight, own_first(adj, feats, first), came)
    out_left, out_right, left, right, *sent = late(
        every, beta, last, index, got, adj, known, weight, (first_left, first_right), crossing
    )

    left = hand_on(left)
    came = [swap(value, *kind) for value, kind in zip(sent, SWAPS)]
    mixed, first_out = own_right(adj, right, first_right, out_left, out_right, after=(handed_left,))
    sent = choose(every, index, got, left)
    right = hand_on(add_received(adj, mixed, came, after=sent[:1]))
    came = [swap(value, *kind) for value, kind in zip(sent, SWAPS)]
    mixed = own_left(adj, left, handed_left, came[:1])
    known = second_known(beta, adj, mixed, right_term(beta, right, weight), weight, came[1:final])
    second_out = second_layer(beta, adj, known, weight, came[final])
    return first_out[None], second_out[None]


def solution(mesh):
    return jax.shard_map(
        shards,
        mesh=mesh,
        in_specs=(
            P("segment", "graph", None),
            P("segment", "graph", None),
            P("graph", None),
            P("segment", None, None),
            P("graph", None, None),
            P("graph", None),
            P("graph"),
            P("graph", None, None, None),
        ),
        out_specs=(P("segment", "graph", None), P("segment", "graph", None)),
        check_vma=False,
    )
```

```python
import functools

import jax
import jax.numpy as jnp
from jax import lax
from jax.experimental import pallas as pl
from jax.experimental.pallas import tpu as pltpu
from jax.sharding import PartitionSpec as P

BLK = 128
REACH = 2
F32 = jnp.float32
BF16 = jnp.bfloat16
SWAPS = ((1, 0), (2, 0), (2, 1), (1, 1))
VMEM = pl.BlockSpec(memory_space=pltpu.VMEM)
SMEM = pl.BlockSpec(memory_space=pltpu.SMEM)
HBM = pl.BlockSpec(memory_space=pltpu.HBM)
ONE = pltpu.SemaphoreType.DMA


def swap(value, stride, phase):
    peers = lax.axis_size("graph")
    pairs = []
    for low in range(peers - stride):
        if (low // stride) % 2 == phase:
            pairs += [(low, low + stride), (low + stride, low)]
    return lax.ppermute(value, "graph", sorted(pairs))


def hand_on(value):
    peers = lax.axis_size("segment")
    return lax.ppermute(value, "segment", [(i, (i + 1) % peers) for i in range(peers)])


def halves(value):
    high = value.astype(BF16)
    return high, (value - high.astype(F32)).astype(BF16)


def dot3(a, b):
    times = functools.partial(jnp.dot, preferred_element_type=F32)
    return times(a[0], b[0]) + (times(a[0], b[1]) + times(a[1], b[0]))


def call(kernel, args, in_specs, outs, flops=0, nbytes=0, scratch=(), after=(), vmem=16):
    count = len(args)

    def body(*refs):
        kernel(*refs[:count], *refs[count + len(after) :])

    return pl.pallas_call(
        body,
        out_shape=outs,
        in_specs=list(in_specs) + [VMEM] * len(after),
        out_specs=tuple(VMEM if isinstance(out, jax.ShapeDtypeStruct) else HBM for out in outs),
        scratch_shapes=list(scratch),
        cost_estimate=pl.CostEstimate(flops=flops, bytes_accessed=nbytes, transcendentals=0),
        compiler_params=pltpu.CompilerParams(vmem_limit_bytes=vmem * 2**20),
    )(*args, *after)


def vmem(*shape, dtype=F32):
    return jax.ShapeDtypeStruct(shape, dtype)


def prepare_kernel(place_ref, slot_ref, count_ref, index_ref, got_ref, last_ref, *refs, kind):
    (vals_ref, feats_ref, first_ref, fresh_ref), refs = refs[:4], refs[4:]
    high_ref, low_ref, sent_ref, left_ref, right_ref, held, total, sem = refs
    half = left_ref.shape[1]
    for mine, origin in ((last_ref[0] == 0, first_ref), (last_ref[0] != 0, fresh_ref)):

        @pl.when(mine)
        def _():
            pltpu.make_async_copy(origin.at[:, :half], left_ref, sem.at[2]).start()
            pltpu.make_async_copy(origin.at[:, half:], right_ref, sem.at[3]).start()

    copies = [pltpu.make_async_copy(vals_ref, held, sem.at[0])]
    row = pl.multiple_of(got_ref[index_ref[kind]] * BLK, BLK)
    copies.append(pltpu.make_async_copy(feats_ref.at[pl.ds(row, BLK)], sent_ref, sem.at[1]))
    for copy in copies:
        copy.start()
    total[...] = jnp.zeros_like(total)
    blocks, most = held.shape[:2]
    copies[0].wait()
    for b in range(blocks):
        for k in range(most):
            slot = slot_ref[b, k]
            past = jnp.maximum(slot - blocks, 0)
            column = jnp.where(slot < blocks, slot, blocks + place_ref[past])
            scale = jnp.where(k < count_ref[b], 0.9, 0.0).astype(F32)
            where = pl.ds(pl.multiple_of(column * BLK, BLK), BLK)
            total[b * BLK : (b + 1) * BLK, where] += scale * held[b, k]
    high, low = halves(total[...])
    high_ref[...] = high
    low_ref[...] = low
    copies[1].wait()
    pltpu.make_async_copy(first_ref.at[:, :half], left_ref, sem.at[2]).wait()
    pltpu.make_async_copy(first_ref.at[:, half:], right_ref, sem.at[3]).wait()


def in_hbm(value):
    return pltpu.with_memory_space_constraint(value, pltpu.HBM)


def prepare(kind, place, slots, counts, index, got, last, vals, feats, first, fresh, after=()):
    rows, width = feats.shape
    span = rows + 2 * REACH * BLK
    return call(
        functools.partial(prepare_kernel, kind=kind),
        (place, slots, counts, index, got[kind], last, *[in_hbm(v) for v in (vals, feats, first, fresh)]),
        [SMEM] * 6 + [HBM] * 4,
        (vmem(rows, span, dtype=BF16),) * 2 + (vmem(BLK, width),) + (vmem(rows, width // 2),) * 2,
        nbytes=4 * vals.size + 4 * rows * span,
        scratch=[pltpu.VMEM(vals.shape, F32), pltpu.VMEM((rows, span), F32), ONE((4,))],
        after=after,
    )


def pick_kernel(index_ref, *refs, kinds):
    count = len(kinds)
    got, source, outs, sem = refs[:count], refs[count], refs[count + 1 : -1], refs[-1]
    copies = []
    for i, kind in enumerate(kinds):
        row = pl.multiple_of(got[i][index_ref[kind]] * BLK, BLK)
        copies.append(pltpu.make_async_copy(source.at[pl.ds(row, BLK)], outs[i], sem.at[i]))
        copies[-1].start()
    for copy in copies:
        copy.wait()


def pick(kinds, index, got, source, after=()):
    return call(
        functools.partial(pick_kernel, kinds=kinds),
        (index, *[got[k] for k in kinds], in_hbm(source)),
        [SMEM] * (1 + len(kinds)) + [HBM],
        (vmem(BLK, source.shape[1]),) * len(kinds),
        nbytes=8 * BLK * source.shape[1] * len(kinds),
        scratch=[ONE((len(kinds),))],
        after=after,
    )


def wanted(kinds, index_ref, got, source_ref, outs):
    for kind, got_ref, out_ref in zip(kinds, got, outs):
        row = pl.multiple_of(got_ref[index_ref[kind]] * BLK, BLK)
        out_ref[...] = source_ref[pl.ds(row, BLK), :]


def choose_kernel(index_ref, *refs, kinds):
    count = len(kinds)
    wanted(kinds, index_ref, refs[:count], refs[count], refs[count + 1 :])


def choose(kinds, index, got, source, after=()):
    return call(
        functools.partial(choose_kernel, kinds=kinds),
        (index, *[got[k] for k in kinds], source),
        [SMEM] * (1 + len(kinds)) + [VMEM],
        (vmem(BLK, source.shape[1]),) * len(kinds),
        nbytes=8 * len(kinds) * BLK * source.shape[1],
        after=after,
    )


def times_adj(high_ref, low_ref, at, value):
    cut = slice(at, at + value.shape[0])
    a, b = (high_ref[:, cut], low_ref[:, cut]), halves(value)
    rows, columns = jnp.concatenate([a[0], a[1], a[0]], axis=1), jnp.concatenate([b[0], b[0], b[1]], axis=0)
    return jnp.dot(rows, columns, preferred_element_type=F32)


def stacked(refs):
    return jnp.concatenate([ref[...] for ref in refs], axis=0)


def mix_kernel(high_ref, low_ref, *refs):
    sources, out_ref, held, sem = refs[:2], refs[2], refs[3:5], refs[5]
    copies = [pltpu.make_async_copy(s, h, sem.at[i]) for i, (s, h) in enumerate(zip(sources, held))]
    for copy in copies:
        copy.start()
    for copy in copies:
        copy.wait()
    out_ref[...] = times_adj(high_ref, low_ref, 0, held[0][...]) + 0.1 * held[1][...]


def own_first(adj, feats, first):
    rows, width = feats.shape
    return call(
        mix_kernel,
        (*adj, in_hbm(feats), in_hbm(first)),
        [VMEM] * 2 + [HBM] * 2,
        (vmem(rows, width),),
        flops=6 * rows * rows * width,
        nbytes=12 * rows * width,
        scratch=[pltpu.VMEM(feats.shape, F32)] * 2 + [ONE((2,))],
    )[0]


def early_kernel(beta_ref, high_ref, low_ref, weight_ref, base_ref, *refs):
    came, out_ref = refs[:-1], refs[-1]
    rows = base_ref.shape[0]
    mixed = base_ref[...] + times_adj(high_ref, low_ref, rows, stacked(came))
    beta = beta_ref[0]
    out_ref[...] = (1.0 - beta) * mixed + beta * dot3(halves(mixed), halves(weight_ref[...]))


def early(beta, adj, weight, base, came):
    rows, width = base.shape
    return call(
        early_kernel,
        (beta, *adj, weight, base, *came),
        [SMEM] + [VMEM] * (4 + len(came)),
        (vmem(rows, width),),
        flops=6 * rows * width * (width + len(came) * BLK),
        nbytes=4 * (width * width + 2 * rows * width),
    )[0]


def late_kernel(beta_ref, last_ref, index_ref, *refs, kinds):
    count = len(kinds)
    got, refs = refs[:count], refs[count:]
    (high_ref, low_ref, base_ref, weight_ref, first_left_ref, first_right_ref, came_ref), refs = refs[:7], refs[7:]
    out_left_ref, out_right_ref, left_ref, right_ref, sent = refs[0], refs[1], refs[2], refs[3], refs[4:]
    half = left_ref.shape[1]
    beta = beta_ref[0]
    last = last_ref[0] != 0
    came = came_ref[...]
    pair = halves(came)
    column = high_ref.shape[1] - BLK
    for at, out_ref, first_ref, next_ref in (
        (half, out_right_ref, first_right_ref, right_ref),
        (0, out_left_ref, first_left_ref, left_ref),
    ):
        cut = slice(at, at + half)
        through = (1.0 - beta) * came[:, cut] + beta * dot3(pair, halves(weight_ref[:, cut]))
        value = jnp.maximum(base_ref[:, cut] + times_adj(high_ref, low_ref, column, through), 0.0)
        out_ref[...] = value
        next_ref[...] = jnp.where(last, first_ref[...], value)
    wanted(kinds, index_ref, got, right_ref, sent)


def late(kinds, beta, last, index, got, adj, base, weight, firsts, came, after=()):
    rows, width = base.shape
    half = width // 2
    return call(
        functools.partial(late_kernel, kinds=kinds),
        (beta, last, index, *[got[k] for k in kinds], *adj, base, weight, *firsts, came),
        [SMEM] * (3 + len(kinds)) + [VMEM] * 7,
        (vmem(rows, half),) * 4 + (vmem(BLK, half),) * len(kinds),
        flops=6 * BLK * width * (width + rows),
        nbytes=4 * width * width + 24 * rows * width,
        after=after,
    )


def right_kernel(high_ref, low_ref, feats_ref, first_ref, left_ref, right_ref, out_ref, handed_ref, sem):
    half = left_ref.shape[1]
    copies = [
        pltpu.make_async_copy(left_ref, handed_ref.at[:, :half], sem.at[0]),
        pltpu.make_async_copy(right_ref, handed_ref.at[:, half:], sem.at[1]),
    ]
    for copy in copies:
        copy.start()
    out_ref[...] = times_adj(high_ref, low_ref, 0, feats_ref[...]) + 0.1 * first_ref[...]
    for copy in copies:
        copy.wait()


def own_right(adj, feats, first, left, right, after=()):
    rows, half = feats.shape
    return call(
        right_kernel,
        (*adj, feats, first, left, right),
        [VMEM] * 6,
        (vmem(rows, half), pltpu.HBM((rows, 2 * half), F32)),
        flops=6 * rows * rows * half,
        nbytes=28 * rows * half,
        scratch=[ONE((2,))],
        after=after,
    )


def left_kernel(high_ref, low_ref, feats_ref, first_ref, *refs):
    came, out_ref = refs[:-1], refs[-1]
    out_ref[...] = times_adj(high_ref, low_ref, 0, stacked((feats_ref, *came))) + 0.1 * first_ref[...]


def own_left(adj, feats, first, came):
    rows, half = feats.shape
    return call(
        left_kernel,
        (*adj, feats, first, *came),
        [VMEM] * (4 + len(came)),
        (vmem(rows, half),),
        flops=6 * rows * rows * half,
        nbytes=12 * rows * half,
    )[0]


def add_kernel(high_ref, low_ref, base_ref, *refs, skip):
    column = base_ref.shape[0] + skip * BLK
    refs[-1][...] = base_ref[...] + times_adj(high_ref, low_ref, column, stacked(refs[:-1]))


def add_received(adj, base, came, skip, after=()):
    rows, width = base.shape
    return call(
        functools.partial(add_kernel, skip=skip),
        (*adj, base, *came),
        [VMEM] * (3 + len(came)),
        (vmem(rows, width),),
        flops=6 * rows * len(came) * BLK * width,
        nbytes=8 * rows * width,
        after=after,
    )[0]


def term_kernel(beta_ref, right_ref, weight_ref, out_ref):
    half = right_ref.shape[1]
    right = right_ref[...]
    beta = beta_ref[0]
    term = beta * dot3(halves(right), halves(weight_ref[half:, :]))
    out_ref[:, :half] = term[:, :half]
    out_ref[:, half:] = term[:, half:] + (1.0 - beta) * right


def right_term(beta, right, weight):
    rows, half = right.shape
    width = weight.shape[1]
    return call(
        term_kernel,
        (beta, right, weight),
        [SMEM] + [VMEM] * 2,
        (vmem(rows, width),),
        flops=6 * rows * half * width,
        nbytes=4 * (half * width + 2 * rows * width),
    )[0]


def known_kernel(beta_ref, high_ref, low_ref, left_ref, term_ref, weight_ref, *refs):
    came, out_ref = refs[:-1], refs[-1]
    rows, half = left_ref.shape
    column = high_ref.shape[1] - BLK - len(came) * BLK
    left = left_ref[...] + times_adj(high_ref, low_ref, column, stacked(came))
    beta = beta_ref[0]
    value = term_ref[...] + beta * dot3(halves(left), halves(weight_ref[:half, :]))
    out_ref[:, :half] = value[:, :half] + (1.0 - beta) * left
    out_ref[:, half:] = value[:, half:]


def second_known(beta, adj, left, term, weight, came):
    rows, half = left.shape
    width = weight.shape[1]
    return call(
        known_kernel,
        (beta, *adj, left, term, weight, *came),
        [SMEM] + [VMEM] * (5 + len(came)),
        (vmem(rows, width),),
        flops=6 * rows * half * (width + len(came) * BLK),
        nbytes=4 * (half * width + 3 * rows * width),
    )[0]


def second_kernel(beta_ref, high_ref, low_ref, base_ref, weight_ref, came_ref, out_ref, held, sem, *, tile):
    half = came_ref.shape[1]
    width = weight_ref.shape[1]
    came = came_ref[...]
    pair = halves(came)
    beta = beta_ref[0]
    column = high_ref.shape[1] - BLK
    copies = []
    for i, at in enumerate(range(0, width, tile)):
        cut = slice(at, at + tile)
        through = beta * dot3(pair, halves(weight_ref[:half, cut]))
        if at < half:
            through = through + (1.0 - beta) * came[:, cut]
        held[:, cut] = jnp.maximum(base_ref[:, cut] + times_adj(high_ref, low_ref, column, through), 0.0)
        copies.append(pltpu.make_async_copy(held.at[:, cut], out_ref.at[:, cut], sem.at[i]))
        copies[-1].start()
    for copy in copies:
        copy.wait()


def second_layer(beta, adj, base, weight, came, tile=256):
    rows, width = base.shape
    half = came.shape[1]
    return call(
        functools.partial(second_kernel, tile=tile),
        (beta, *adj, base, weight, came),
        [SMEM] + [VMEM] * 5,
        (pltpu.HBM((rows, width), F32),),
        flops=6 * BLK * width * (half + rows),
        nbytes=4 * (half * width + 3 * rows * width),
        scratch=[pltpu.VMEM((rows, width), F32), ONE((width // tile,))],
    )[0]


def shards(state, initial, fresh, weights, wants, adj_slot, adj_count, adj_vals):
    section = lax.axis_index("segment")
    part = lax.axis_index("graph")
    beta = jnp.log(0.5 / (section.astype(F32) + 1.0) + 1.0).reshape(1)
    last = (section == lax.axis_size("segment") - 1).astype(jnp.int32).reshape(1)
    feats, first, weight = state[0], initial[0], weights[0]
    half = feats.shape[1] // 2
    asks = wants.reshape(wants.shape[1])

    place = []
    for position in range(2 * REACH):
        stride = position // 2 + 1
        low = (part // stride) % 2 == 0
        phase = jnp.where(low, 1 - position % 2, position % 2)
        place.append(jnp.where(phase == 0, SWAPS.index((stride, 0)), SWAPS.index((stride, 1))))
    place = jnp.stack(place).astype(jnp.int32)
    index = []
    for stride, phase in SWAPS:
        low = (part // stride) % 2 == phase
        index.append(jnp.where(low, 2 * stride - 2, 2 * stride - 1))
    index = jnp.stack(index).astype(jnp.int32)

    got = [swap(asks, *kind) for kind in SWAPS]
    final = len(SWAPS) - 1
    others = tuple(range(final))
    every = tuple(range(len(SWAPS)))

    sent = pick(others, index, got, feats, after=got[final:])
    came = [swap(value, *SWAPS[k]) for k, value in enumerate(sent)]
    *adj, sent, first_left, first_right = prepare(
        final, place, adj_slot, adj_count, index, got, last, adj_vals, feats, first, fresh, after=sent[:1]
    )
    crossing = swap(sent, *SWAPS[final])
    handed_left = hand_on(first_left)
    known = early(beta, adj, weight, own_first(adj, feats, first), came)
    out_left, out_right, left, right, *sent = late(
        every, beta, last, index, got, adj, known, weight, (first_left, first_right), crossing
    )

    left = hand_on(left)
    came = [swap(value, *kind) for value, kind in zip(sent, SWAPS)]
    mixed, first_out = own_right(adj, right, first_right, out_left, out_right, after=(handed_left,))
    sent = choose(every, index, got, left)
    mixed = add_received(adj, mixed, came[:final], 0)
    right = hand_on(add_received(adj, mixed, came[final:], final, after=sent[:1]))
    came = [swap(value, *kind) for value, kind in zip(sent, SWAPS)]
    mixed = own_left(adj, left, handed_left, came[:1])
    known = second_known(beta, adj, mixed, right_term(beta, right, weight), weight, came[1:final])
    second_out = second_layer(beta, adj, known, weight, came[final])
    return first_out[None], second_out[None]


def solution(mesh):
    return jax.shard_map(
        shards,
        mesh=mesh,
        in_specs=(
            P("segment", "graph", None),
            P("segment", "graph", None),
            P("graph", None),
            P("segment", None, None),
            P("graph", None, None),
            P("graph", None),
            P("graph"),
            P("graph", None, None, None),
        ),
        out_specs=(P("segment", "graph", None), P("segment", "graph", None)),
        check_vma=False,
    )
```

```python
import functools

import jax
import jax.numpy as jnp
from jax import lax
from jax.experimental import pallas as pl
from jax.experimental.pallas import tpu as pltpu
from jax.sharding import PartitionSpec as P

BLK = 128
REACH = 2
F32 = jnp.float32
BF16 = jnp.bfloat16
SWAPS = ((1, 0), (2, 0), (2, 1), (1, 1))
VMEM = pl.BlockSpec(memory_space=pltpu.VMEM)
SMEM = pl.BlockSpec(memory_space=pltpu.SMEM)
HBM = pl.BlockSpec(memory_space=pltpu.HBM)
ONE = pltpu.SemaphoreType.DMA


def swap(value, stride, phase):
    peers = lax.axis_size("graph")
    pairs = []
    for low in range(peers - stride):
        if (low // stride) % 2 == phase:
            pairs += [(low, low + stride), (low + stride, low)]
    return lax.ppermute(value, "graph", sorted(pairs))


def hand_on(value):
    peers = lax.axis_size("segment")
    return lax.ppermute(value, "segment", [(i, (i + 1) % peers) for i in range(peers)])


def halves(value):
    high = value.astype(BF16)
    return high, (value - high.astype(F32)).astype(BF16)


def dot3(a, b):
    times = functools.partial(jnp.dot, preferred_element_type=F32)
    return times(a[0], b[0]) + (times(a[0], b[1]) + times(a[1], b[0]))


def call(kernel, args, in_specs, outs, flops=0, nbytes=0, scratch=(), after=(), vmem=16):
    count = len(args)

    def body(*refs):
        kernel(*refs[:count], *refs[count + len(after) :])

    return pl.pallas_call(
        body,
        out_shape=outs,
        in_specs=list(in_specs) + [VMEM] * len(after),
        out_specs=tuple(VMEM if isinstance(out, jax.ShapeDtypeStruct) else HBM for out in outs),
        scratch_shapes=list(scratch),
        cost_estimate=pl.CostEstimate(flops=flops, bytes_accessed=nbytes, transcendentals=0),
        compiler_params=pltpu.CompilerParams(vmem_limit_bytes=vmem * 2**20),
    )(*args, *after)


def vmem(*shape, dtype=F32):
    return jax.ShapeDtypeStruct(shape, dtype)


def prepare_kernel(place_ref, slot_ref, count_ref, index_ref, got_ref, last_ref, *refs, kind):
    (vals_ref, feats_ref, first_ref, fresh_ref), refs = refs[:4], refs[4:]
    high_ref, low_ref, sent_ref, left_ref, right_ref, held, total, sem = refs
    half = left_ref.shape[1]
    for mine, origin in ((last_ref[0] == 0, first_ref), (last_ref[0] != 0, fresh_ref)):

        @pl.when(mine)
        def _():
            pltpu.make_async_copy(origin.at[:, :half], left_ref, sem.at[2]).start()
            pltpu.make_async_copy(origin.at[:, half:], right_ref, sem.at[3]).start()

    copies = [pltpu.make_async_copy(vals_ref, held, sem.at[0])]
    row = pl.multiple_of(got_ref[index_ref[kind]] * BLK, BLK)
    copies.append(pltpu.make_async_copy(feats_ref.at[pl.ds(row, BLK)], sent_ref, sem.at[1]))
    for copy in copies:
        copy.start()
    total[...] = jnp.zeros_like(total)
    blocks, most = held.shape[:2]
    copies[0].wait()
    for b in range(blocks):
        for k in range(most):
            slot = slot_ref[b, k]
            past = jnp.maximum(slot - blocks, 0)
            column = jnp.where(slot < blocks, slot, blocks + place_ref[past])
            scale = jnp.where(k < count_ref[b], 0.9, 0.0).astype(F32)
            where = pl.ds(pl.multiple_of(column * BLK, BLK), BLK)
            total[b * BLK : (b + 1) * BLK, where] += scale * held[b, k]
    high, low = halves(total[...])
    high_ref[...] = high
    low_ref[...] = low
    copies[1].wait()
    pltpu.make_async_copy(first_ref.at[:, :half], left_ref, sem.at[2]).wait()
    pltpu.make_async_copy(first_ref.at[:, half:], right_ref, sem.at[3]).wait()


def in_hbm(value):
    return pltpu.with_memory_space_constraint(value, pltpu.HBM)


def prepare(kind, place, slots, counts, index, got, last, vals, feats, first, fresh, after=()):
    rows, width = feats.shape
    span = rows + 2 * REACH * BLK
    return call(
        functools.partial(prepare_kernel, kind=kind),
        (place, slots, counts, index, got[kind], last, *[in_hbm(v) for v in (vals, feats, first, fresh)]),
        [SMEM] * 6 + [HBM] * 4,
        (vmem(rows, span, dtype=BF16),) * 2 + (vmem(BLK, width),) + (vmem(rows, width // 2),) * 2,
        nbytes=4 * vals.size + 4 * rows * span,
        scratch=[pltpu.VMEM(vals.shape, F32), pltpu.VMEM((rows, span), F32), ONE((4,))],
        after=after,
    )


def pick_kernel(index_ref, *refs, kinds):
    count = len(kinds)
    got, source, outs, sem = refs[:count], refs[count], refs[count + 1 : -1], refs[-1]
    copies = []
    for i, kind in enumerate(kinds):
        row = pl.multiple_of(got[i][index_ref[kind]] * BLK, BLK)
        copies.append(pltpu.make_async_copy(source.at[pl.ds(row, BLK)], outs[i], sem.at[i]))
        copies[-1].start()
    for copy in copies:
        copy.wait()


def pick(kinds, index, got, source, after=()):
    return call(
        functools.partial(pick_kernel, kinds=kinds),
        (index, *[got[k] for k in kinds], in_hbm(source)),
        [SMEM] * (1 + len(kinds)) + [HBM],
        (vmem(BLK, source.shape[1]),) * len(kinds),
        nbytes=8 * BLK * source.shape[1] * len(kinds),
        scratch=[ONE((len(kinds),))],
        after=after,
    )


def wanted(kinds, index_ref, got, source_ref, outs):
    for kind, got_ref, out_ref in zip(kinds, got, outs):
        row = pl.multiple_of(got_ref[index_ref[kind]] * BLK, BLK)
        out_ref[...] = source_ref[pl.ds(row, BLK), :]


def choose_kernel(index_ref, *refs, kinds):
    count = len(kinds)
    wanted(kinds, index_ref, refs[:count], refs[count], refs[count + 1 :])


def choose(kinds, index, got, source, after=()):
    return call(
        functools.partial(choose_kernel, kinds=kinds),
        (index, *[got[k] for k in kinds], source),
        [SMEM] * (1 + len(kinds)) + [VMEM],
        (vmem(BLK, source.shape[1]),) * len(kinds),
        nbytes=8 * len(kinds) * BLK * source.shape[1],
        after=after,
    )


def times_adj(high_ref, low_ref, at, value):
    cut = slice(at, at + value.shape[0])
    a, b = (high_ref[:, cut], low_ref[:, cut]), halves(value)
    rows, columns = jnp.concatenate([a[0], a[1], a[0]], axis=1), jnp.concatenate([b[0], b[0], b[1]], axis=0)
    return jnp.dot(rows, columns, preferred_element_type=F32)


def stacked(refs):
    return jnp.concatenate([ref[...] for ref in refs], axis=0)


def mix_kernel(high_ref, low_ref, *refs):
    sources, out_ref, held, sem = refs[:2], refs[2], refs[3:5], refs[5]
    copies = [pltpu.make_async_copy(s, h, sem.at[i]) for i, (s, h) in enumerate(zip(sources, held))]
    for copy in copies:
        copy.start()
    for copy in copies:
        copy.wait()
    out_ref[...] = times_adj(high_ref, low_ref, 0, held[0][...]) + 0.1 * held[1][...]


def own_first(adj, feats, first):
    rows, width = feats.shape
    return call(
        mix_kernel,
        (*adj, in_hbm(feats), in_hbm(first)),
        [VMEM] * 2 + [HBM] * 2,
        (vmem(rows, width),),
        flops=6 * rows * rows * width,
        nbytes=12 * rows * width,
        scratch=[pltpu.VMEM(feats.shape, F32)] * 2 + [ONE((2,))],
    )[0]


def early_kernel(beta_ref, high_ref, low_ref, weight_ref, base_ref, *refs):
    came, out_ref = refs[:-1], refs[-1]
    rows = base_ref.shape[0]
    mixed = base_ref[...] + times_adj(high_ref, low_ref, rows, stacked(came))
    beta = beta_ref[0]
    out_ref[...] = (1.0 - beta) * mixed + beta * dot3(halves(mixed), halves(weight_ref[...]))


def early(beta, adj, weight, base, came):
    rows, width = base.shape
    return call(
        early_kernel,
        (beta, *adj, weight, base, *came),
        [SMEM] + [VMEM] * (4 + len(came)),
        (vmem(rows, width),),
        flops=6 * rows * width * (width + len(came) * BLK),
        nbytes=4 * (width * width + 2 * rows * width),
    )[0]


def late_kernel(beta_ref, last_ref, index_ref, *refs, kinds):
    count = len(kinds)
    got, refs = refs[:count], refs[count:]
    (high_ref, low_ref, base_ref, weight_ref, first_left_ref, first_right_ref, came_ref), refs = refs[:7], refs[7:]
    out_left_ref, out_right_ref, left_ref, right_ref, sent = refs[0], refs[1], refs[2], refs[3], refs[4:]
    half = left_ref.shape[1]
    beta = beta_ref[0]
    last = last_ref[0] != 0
    came = came_ref[...]
    pair = halves(came)
    column = high_ref.shape[1] - BLK
    for at, out_ref, first_ref, next_ref in (
        (half, out_right_ref, first_right_ref, right_ref),
        (0, out_left_ref, first_left_ref, left_ref),
    ):
        cut = slice(at, at + half)
        through = (1.0 - beta) * came[:, cut] + beta * dot3(pair, halves(weight_ref[:, cut]))
        value = jnp.maximum(base_ref[:, cut] + times_adj(high_ref, low_ref, column, through), 0.0)
        out_ref[...] = value
        next_ref[...] = jnp.where(last, first_ref[...], value)
    wanted(kinds, index_ref, got, right_ref, sent)


def late(kinds, beta, last, index, got, adj, base, weight, firsts, came, after=()):
    rows, width = base.shape
    half = width // 2
    return call(
        functools.partial(late_kernel, kinds=kinds),
        (beta, last, index, *[got[k] for k in kinds], *adj, base, weight, *firsts, came),
        [SMEM] * (3 + len(kinds)) + [VMEM] * 7,
        (vmem(rows, half),) * 4 + (vmem(BLK, half),) * len(kinds),
        flops=6 * BLK * width * (width + rows),
        nbytes=4 * width * width + 24 * rows * width,
        after=after,
    )


def right_kernel(high_ref, low_ref, feats_ref, first_ref, left_ref, right_ref, out_ref, handed_ref, sem):
    half = left_ref.shape[1]
    copies = [
        pltpu.make_async_copy(left_ref, handed_ref.at[:, :half], sem.at[0]),
        pltpu.make_async_copy(right_ref, handed_ref.at[:, half:], sem.at[1]),
    ]
    for copy in copies:
        copy.start()
    out_ref[...] = times_adj(high_ref, low_ref, 0, feats_ref[...]) + 0.1 * first_ref[...]
    for copy in copies:
        copy.wait()


def own_right(adj, feats, first, left, right, after=()):
    rows, half = feats.shape
    return call(
        right_kernel,
        (*adj, feats, first, left, right),
        [VMEM] * 6,
        (vmem(rows, half), pltpu.HBM((rows, 2 * half), F32)),
        flops=6 * rows * rows * half,
        nbytes=28 * rows * half,
        scratch=[ONE((2,))],
        after=after,
    )


def left_kernel(high_ref, low_ref, feats_ref, first_ref, *refs):
    came, out_ref = refs[:-1], refs[-1]
    out_ref[...] = times_adj(high_ref, low_ref, 0, stacked((feats_ref, *came))) + 0.1 * first_ref[...]


def own_left(adj, feats, first, came):
    rows, half = feats.shape
    return call(
        left_kernel,
        (*adj, feats, first, *came),
        [VMEM] * (4 + len(came)),
        (vmem(rows, half),),
        flops=6 * rows * rows * half,
        nbytes=12 * rows * half,
    )[0]


def add_kernel(high_ref, low_ref, base_ref, *refs, skip):
    column = base_ref.shape[0] + skip * BLK
    refs[-1][...] = base_ref[...] + times_adj(high_ref, low_ref, column, stacked(refs[:-1]))


def add_received(adj, base, came, skip, after=()):
    rows, width = base.shape
    return call(
        functools.partial(add_kernel, skip=skip),
        (*adj, base, *came),
        [VMEM] * (3 + len(came)),
        (vmem(rows, width),),
        flops=6 * rows * len(came) * BLK * width,
        nbytes=8 * rows * width,
        after=after,
    )[0]


def term_kernel(beta_ref, right_ref, weight_ref, out_ref):
    half = right_ref.shape[1]
    right = right_ref[...]
    beta = beta_ref[0]
    term = beta * dot3(halves(right), halves(weight_ref[half:, :]))
    out_ref[:, :half] = term[:, :half]
    out_ref[:, half:] = term[:, half:] + (1.0 - beta) * right


def right_term(beta, right, weight):
    rows, half = right.shape
    width = weight.shape[1]
    return call(
        term_kernel,
        (beta, right, weight),
        [SMEM] + [VMEM] * 2,
        (vmem(rows, width),),
        flops=6 * rows * half * width,
        nbytes=4 * (half * width + 2 * rows * width),
    )[0]


def known_kernel(beta_ref, high_ref, low_ref, left_ref, term_ref, weight_ref, *refs):
    came, out_ref = refs[:-1], refs[-1]
    rows, half = left_ref.shape
    column = high_ref.shape[1] - BLK - len(came) * BLK
    left = left_ref[...] + times_adj(high_ref, low_ref, column, stacked(came))
    beta = beta_ref[0]
    value = term_ref[...] + beta * dot3(halves(left), halves(weight_ref[:half, :]))
    out_ref[:, :half] = value[:, :half] + (1.0 - beta) * left
    out_ref[:, half:] = value[:, half:]


def second_known(beta, adj, left, term, weight, came):
    rows, half = left.shape
    width = weight.shape[1]
    return call(
        known_kernel,
        (beta, *adj, left, term, weight, *came),
        [SMEM] + [VMEM] * (5 + len(came)),
        (vmem(rows, width),),
        flops=6 * rows * half * (width + len(came) * BLK),
        nbytes=4 * (half * width + 3 * rows * width),
    )[0]


def second_kernel(beta_ref, high_ref, low_ref, base_ref, weight_ref, came_ref, out_ref, held, sem, *, tile):
    half = came_ref.shape[1]
    width = weight_ref.shape[1]
    came = came_ref[...]
    pair = halves(came)
    beta = beta_ref[0]
    column = high_ref.shape[1] - BLK
    copies = []
    for i, at in enumerate(range(0, width, tile)):
        cut = slice(at, at + tile)
        through = beta * dot3(pair, halves(weight_ref[:half, cut]))
        if at < half:
            through = through + (1.0 - beta) * came[:, cut]
        held[:, cut] = jnp.maximum(base_ref[:, cut] + times_adj(high_ref, low_ref, column, through), 0.0)
        copies.append(pltpu.make_async_copy(held.at[:, cut], out_ref.at[:, cut], sem.at[i]))
        copies[-1].start()
    for copy in copies:
        copy.wait()


def second_layer(beta, adj, base, weight, came, tile=512):
    rows, width = base.shape
    half = came.shape[1]
    return call(
        functools.partial(second_kernel, tile=tile),
        (beta, *adj, base, weight, came),
        [SMEM] + [VMEM] * 5,
        (pltpu.HBM((rows, width), F32),),
        flops=6 * BLK * width * (half + rows),
        nbytes=4 * (half * width + 3 * rows * width),
        scratch=[pltpu.VMEM((rows, width), F32), ONE((width // tile,))],
    )[0]


def shards(state, initial, fresh, weights, wants, adj_slot, adj_count, adj_vals):
    section = lax.axis_index("segment")
    part = lax.axis_index("graph")
    beta = jnp.log(0.5 / (section.astype(F32) + 1.0) + 1.0).reshape(1)
    last = (section == lax.axis_size("segment") - 1).astype(jnp.int32).reshape(1)
    feats, first, weight = state[0], initial[0], weights[0]
    half = feats.shape[1] // 2
    asks = wants.reshape(wants.shape[1])

    place = []
    for position in range(2 * REACH):
        stride = position // 2 + 1
        low = (part // stride) % 2 == 0
        phase = jnp.where(low, 1 - position % 2, position % 2)
        place.append(jnp.where(phase == 0, SWAPS.index((stride, 0)), SWAPS.index((stride, 1))))
    place = jnp.stack(place).astype(jnp.int32)
    index = []
    for stride, phase in SWAPS:
        low = (part // stride) % 2 == phase
        index.append(jnp.where(low, 2 * stride - 2, 2 * stride - 1))
    index = jnp.stack(index).astype(jnp.int32)

    got = [swap(asks, *kind) for kind in SWAPS]
    final = len(SWAPS) - 1
    others = tuple(range(final))
    every = tuple(range(len(SWAPS)))

    sent = pick(others, index, got, feats, after=got[final:])
    came = [swap(value, *SWAPS[k]) for k, value in enumerate(sent)]
    *adj, sent, first_left, first_right = prepare(
        final, place, adj_slot, adj_count, index, got, last, adj_vals, feats, first, fresh, after=sent[:1]
    )
    crossing = swap(sent, *SWAPS[final])
    handed_left = hand_on(first_left)
    known = early(beta, adj, weight, own_first(adj, feats, first), came)
    out_left, out_right, left, right, *sent = late(
        every, beta, last, index, got, adj, known, weight, (first_left, first_right), crossing
    )

    left = hand_on(left)
    came = [swap(value, *kind) for value, kind in zip(sent, SWAPS)]
    mixed, first_out = own_right(adj, right, first_right, out_left, out_right, after=(handed_left,))
    sent = choose(every, index, got, left)
    mixed = add_received(adj, mixed, came[:final], 0)
    right = hand_on(add_received(adj, mixed, came[final:], final, after=sent[:1]))
    came = [swap(value, *kind) for value, kind in zip(sent, SWAPS)]
    mixed = own_left(adj, left, handed_left, came[:1])
    known = second_known(beta, adj, mixed, right_term(beta, right, weight), weight, came[1:final])
    second_out = second_layer(beta, adj, known, weight, came[final])
    return first_out[None], second_out[None]


def solution(mesh):
    return jax.shard_map(
        shards,
        mesh=mesh,
        in_specs=(
            P("segment", "graph", None),
            P("segment", "graph", None),
            P("graph", None),
            P("segment", None, None),
            P("graph", None, None),
            P("graph", None),
            P("graph"),
            P("graph", None, None, None),
        ),
        out_specs=(P("segment", "graph", None), P("segment", "graph", None)),
        check_vma=False,
    )
```
